32 devices in a mesh: parts: 2 (over y), tensor: 4 (over z), dp: 4 (over x, core).
Axes of the slice: x: 2, y: 2, z: 4, core: 2. Of those that a mesh axis runs over, the one named last changes fastest.
Arguments:
- tokens: bfloat16 [1024, 8192], P(('parts', 'dp'), 'tensor'), parts along dimension 0, may hold values from -6 to 6
- weight: bfloat16 [8192, 8192], P(None, 'tensor'), may hold values from -0.0625 to 0.0625
- adapter_down_factor: bfloat16 [8, 8192, 256], P(('parts', 'dp'), 'tensor'), parts along dimension 0, may hold values from -0.0625 to 0.0625
- adapter_up_factor: bfloat16 [8, 256, 8192], P(('parts', 'dp'), None, 'tensor'), parts along dimension 0, may hold values from -0.375 to 0.375
- cotangent: bfloat16 [1024, 8192], P(('parts', 'dp'), 'tensor'), parts along dimension 0, may hold values from -6 to 6
- micro_destination_group: int32 [64, 1], P('parts'), parts along dimension 0, may hold values from 0 to 3; in each aligned block of 8 rows (0 to 7, 8 to 15, ...) at most 2 rows name the same one
- micro_adapter: int32 [64], P('parts'), parts along dimension 0, may hold values from 0 to 3
- micro_token_count: int32 [64], P('parts'), parts along dimension 0, may hold values from 12 to 16
- adapter_rank_bucket: int32 [8], P('parts'), parts along dimension 0, may hold values from 0 to 2, as said below
- adapter_home_row: int32 [8], P('parts'), parts along dimension 0, may hold values from 0 to 3, each once
Outputs:
- outputs: bfloat16 [1024, 8192], P(('parts', 'dp'), 'tensor'), parts along dimension 0
- packed_input_gradient: bfloat16 [1024, 8192], P(('parts', 'dp'), 'tensor'), parts along dimension 0
- grad_a: bfloat16 [8, 8192, 256], P(('parts', 'dp'), 'tensor'), parts along dimension 0
- grad_b: bfloat16 [8, 256, 8192], P(('parts', 'dp'), None, 'tensor'), parts along dimension 0
The draws below stay inside these ranges and needn't reach their ends.
There are 2 independent parts, one for each index of `parts`. The reference program is written for one: setup_inputs(seed, part) draws one part's arguments, and reference() takes and returns one part's arrays. A program takes and returns all parts, laid end to end along the dimension named above; an argument that names none is the same for every part. Nothing has to cross between parts.
Inputs may be any that keep to these rules, and one draw needn't show every extreme that they name: `micro_destination_group`: within the 8 micro-batches of one source group no destination group is named more than 2 times. `micro_token_count`: tokens 0 to count - 1 of a micro-batch are live. `adapter_rank_bucket`: an adapter's rank is 16 times 4 to the power of its bucket. `adapter_home_row`: A permutation.
All inputs are finite; a program needn't handle non-finite values.
Results may differ from the reference program's by a relative error of at most 0.015.
Values may be sent and summed in bfloat16 or wider, within the bound.
A program may use at most 192 MiB of HBM per device.

```python
import math
import jax
import jax.numpy as jnp
import numpy as np
from jax import lax

MODEL_WIDTH = 8192
RANK_LOW = 16
LARGEST_RANK = 256
CAP = 2
MICRO_TOKENS = 16
MB_DEV = 8
ADAPTER_COUNT = 4
TOKENS = 512
PACKED = 512
N_TENSOR = 4
N_DP = 4


def draw_adapter_rank_bucket(key, part):
    key = jax.random.fold_in(key, 7)
    order = jax.random.permutation(key, jnp.arange(ADAPTER_COUNT, dtype=jnp.int32))
    return (order % 3).astype(jnp.int32)


def with_ends(values, own_key, smallest, top_value):
    spot = [jax.random.randint(jax.random.fold_in(own_key, axis), (), 0, length) for axis, length in enumerate(values.shape)]
    longest = values.shape.index(max(values.shape))
    beside = spot[:longest] + [(spot[longest] + 1) % values.shape[longest]] + spot[longest + 1:]
    return values.at[tuple(spot)].set(smallest).at[tuple(beside)].set(top_value)


def levels(own_key, extent, pieces, low, top_value):
    def one(axis_at, shards_of):
        draws = jax.random.uniform(jax.random.fold_in(jax.random.fold_in(own_key, 6), axis_at), (shards_of,), jnp.float32, low / len(pieces), top_value / len(pieces))
        return jnp.repeat(jnp.exp(draws), extent[axis_at] // shards_of).reshape((-1,) + (1,) * (len(extent) - axis_at - 1))

    loudness = one(*pieces[0])
    for cut in pieces[1:]:
        loudness = loudness * one(*cut)
    return loudness


def rank_table(number_of, lean):
    portions = [(1 << 20) // math.isqrt(rank ** lean) + 1 for rank in range(1, number_of + 1)]
    spread = 1 + sum(portions) // (1 << 30)
    return np.cumsum(np.array([max(1, weight // spread) for weight in portions]))


def skewed_ids(stream_key, shape, count, skew):
    listing = rank_table(count, skew)
    ticket = jax.random.randint(jax.random.fold_in(stream_key, 1), shape, 0, int(listing[count - 1]))
    rank = jnp.searchsorted(jnp.asarray(listing, jnp.int32), ticket, side="right")
    return jax.random.permutation(jax.random.fold_in(stream_key, 2), count)[rank].astype(jnp.int32)


def deal_out(own_key, own, number, rows, count, top, most, slope):
    order = jax.random.permutation(own_key, count)
    crowded, ordinary = shares(count, rows * top, most, slope, True), shares(count, rows * top, most, slope, False)
    places = jnp.arange(count)

    def named(lengths, offset_by):
        used = int((lengths > 0).sum())
        fixed = max(1, used // 4)
        moved = fixed + (places - fixed + offset_by * (used - fixed)) % max(1, count - fixed)
        return jnp.zeros((count,), jnp.int32).at[order[jnp.where(places < fixed, places, moved)]].set(jnp.asarray(lengths, jnp.int32))

    lengths = jnp.where(number % 4 == 0, named(crowded, number // 4), named(ordinary, number - number // 4 - 1))
    mixed = jax.random.permutation(jax.random.fold_in(own, 3), count)
    giver, sink = mixed[0:count // 2 * 2:2], mixed[1:count // 2 * 2:2]
    margin = jnp.minimum(lengths[giver] - 1, most - lengths[sink]) // 2
    margin = jnp.where((giver == order[0]) | (sink == order[0]) | (lengths[sink] == 0), 0, jnp.maximum(margin, 0))
    moved = jax.random.randint(jax.random.fold_in(own, 4), (count // 2,), 0, 1 << 20) % (margin + 1)
    lengths = lengths.at[giver].add(-moved).at[sink].add(moved)
    items = jnp.searchsorted(jnp.cumsum(lengths), jnp.arange(rows * top), side="right").astype(jnp.int32)
    listing = items.reshape(top, rows).T
    listing = listing[jax.random.permutation(jax.random.fold_in(own, 1), rows)]
    offset_by = jax.random.randint(jax.random.fold_in(own, 2), (rows, 1), 0, top)
    return jnp.take_along_axis(listing, (jnp.arange(top)[None, :] + offset_by) % top, axis=1)


def shares(count, total, bound, skew, full):
    weights = [(1 << 20) // math.isqrt(standing ** skew) + 1 for standing in range(1, count + 1)]
    largest = bound if full else min(bound, max(-(-total // count), total * weights[0] // sum(weights)))
    least = 1 if total - largest >= count - 1 else 0
    given, surplus = [largest] + [least] * (count - 1), total - largest - least * (count - 1)
    while surplus > 0:
        free = [i for i in range(1, count) if given[i] < largest] or [i for i in range(1, count) if given[i] < bound]
        whole, left = sum([weights[i] for i in free]), surplus
        for i in free:
            extra = min(bound - given[i], max(1, left * weights[i] // whole), surplus)
            given[i] = given[i] + extra
            surplus = surplus - extra
    return np.array(given)


def gaussian(rng, shape, scale, reach, split=(), held_as=jnp.bfloat16):
    loudness = levels(rng, shape, split, -0.22, 0.18) if split else 1.0
    array = jax.random.normal(rng, shape, jnp.float32) * scale * loudness
    return jnp.minimum(jnp.maximum(array, -reach), reach).astype(held_as)


def setup_inputs(seed: int = 0, part: int = 0) -> dict:
    key_of = jax.random.split(jax.random.key(seed), 11)
    part_keys = jax.random.split(jax.random.fold_in(key_of[10], part), 11)
    tokens = gaussian(part_keys[0], (TOKENS, MODEL_WIDTH), 1.0, 6.0, ((0, 4), (1, 4)))
    weight = gaussian(key_of[1], (MODEL_WIDTH, MODEL_WIDTH), MODEL_WIDTH ** -0.5, 0.0625, ((1, 4),))
    adapter_down_factor = gaussian(part_keys[2], (ADAPTER_COUNT, MODEL_WIDTH, LARGEST_RANK), MODEL_WIDTH ** -0.5, 0.0625, ((0, 4), (1, 4)))
    adapter_up_factor = gaussian(part_keys[3], (ADAPTER_COUNT, LARGEST_RANK, MODEL_WIDTH), LARGEST_RANK ** -0.5, 0.375, ((0, 4), (2, 4)))
    cotangent = gaussian(part_keys[4], (PACKED, MODEL_WIDTH), 1.0, 6.0, ((0, 4), (1, 4)))
    micro_destination_group_keys = jax.random.split(jax.random.fold_in(part_keys[5], 1), (N_DP * MB_DEV) // MB_DEV)
    micro_destination_group_turns = jax.random.permutation(jax.random.fold_in(part_keys[5], 3), (N_DP * MB_DEV) // MB_DEV)
    micro_destination_group = jax.vmap(lambda own, number: deal_out(jax.random.fold_in(part_keys[5], 2), own, number, MB_DEV, N_DP, 1, CAP, 2))(micro_destination_group_keys, micro_destination_group_turns).reshape((N_DP * MB_DEV, 1))
    micro_adapter = with_ends(skewed_ids(part_keys[6], (N_DP * MB_DEV,), ADAPTER_COUNT, 2), jax.random.fold_in(part_keys[6], 3), 0, ADAPTER_COUNT - 1).astype(jnp.int32)
    micro_token_count = with_ends(jax.random.randint(part_keys[7], (N_DP * MB_DEV,), 3 * MICRO_TOKENS // 4, MICRO_TOKENS + 1), jax.random.fold_in(part_keys[7], 1), 3 * MICRO_TOKENS // 4, MICRO_TOKENS).astype(jnp.int32)
    adapter_rank_bucket = draw_adapter_rank_bucket(jax.random.fold_in(jax.random.fold_in(key_of[10], part), 71), part)
    adapter_home_row = jax.random.permutation(part_keys[9], ADAPTER_COUNT).astype(jnp.int32)
    return {"tokens": tokens, "weight": weight, "adapter_down_factor": adapter_down_factor, "adapter_up_factor": adapter_up_factor, "cotangent": cotangent, "micro_destination_group": micro_destination_group, "micro_adapter": micro_adapter, "micro_token_count": micro_token_count, "adapter_rank_bucket": adapter_rank_bucket, "adapter_home_row": adapter_home_row}


def packing_plan(micro_destination_group, micro_adapter, micro_token_count, n_groups, per_group):
    groups = micro_destination_group[:, 0]
    count_all = groups.shape[0]
    indices = jnp.arange(count_all, dtype=jnp.int32)
    source = indices // per_group
    earlier = (groups[:, None] == groups[None, :]) & (source[:, None] == source[None, :]) & (indices[None, :] < indices[:, None])
    placing = lax.optimization_barrier(jnp.sum(earlier.astype(jnp.int32), axis=1))
    target = groups * (n_groups * CAP) + source * CAP + placing
    slot_ids = jnp.arange(n_groups * n_groups * CAP, dtype=jnp.int32)
    select = (target[None, :] == slot_ids[:, None]).astype(jnp.int32)
    present = lax.optimization_barrier(jnp.sum(select, axis=1))
    anchor = lax.optimization_barrier(jnp.sum(select * indices[None, :], axis=1))
    adapter = lax.optimization_barrier(jnp.sum(select * micro_adapter[None, :], axis=1))
    counted = lax.optimization_barrier(jnp.sum(select * micro_token_count[None, :], axis=1))
    return (present, anchor, adapter, counted)

def slot_terms(adapter, counted, adapter_rank_bucket, adapter_home_row):
    table_ids = jnp.arange(adapter_home_row.shape[0], dtype=jnp.int32)
    matches = (adapter[:, None] == table_ids[None, :]).astype(jnp.int32)
    factor_storage = lax.optimization_barrier(jnp.sum(matches * adapter_home_row[None, :], axis=1))
    bucket = lax.optimization_barrier(jnp.sum(matches * adapter_rank_bucket[None, :], axis=1))
    rank_size = RANK_LOW * jnp.where(bucket == 0, 1, jnp.where(bucket == 1, 4, 16))
    adapter_scale = jnp.sqrt(LARGEST_RANK / rank_size.astype(jnp.float32))
    column_mask = (jnp.arange(LARGEST_RANK, dtype=jnp.int32)[None, :] < rank_size[:, None]).astype(jnp.float32)
    live = (jnp.arange(MICRO_TOKENS, dtype=jnp.int32)[None, :] < counted[:, None]).astype(jnp.float32)
    return (factor_storage, adapter_scale, column_mask, live)

def reference(tokens, weight, adapter_down_factor, adapter_up_factor, cotangent, micro_destination_group, micro_adapter, micro_token_count, adapter_rank_bucket, adapter_home_row):
    present, anchor, adapter, counted = packing_plan(micro_destination_group, micro_adapter, micro_token_count, N_DP, MB_DEV)
    factor_storage, adapter_scale, column_mask, live = slot_terms(adapter, counted, adapter_rank_bucket, adapter_home_row)
    slot_count = N_DP * N_DP * CAP
    micro = tokens.reshape(N_DP * MB_DEV, MICRO_TOKENS, MODEL_WIDTH)
    packed_tokens = jnp.where(present[:, None, None] > 0, micro[anchor], jnp.zeros((), jnp.bfloat16))
    masked_values = cotangent.reshape(slot_count, MICRO_TOKENS, MODEL_WIDTH) * live[:, :, None].astype(jnp.bfloat16)
    flat_in = packed_tokens.reshape(-1, MODEL_WIDTH)
    flat_dy = masked_values.reshape(-1, MODEL_WIDTH)
    frozen_output = jnp.dot(flat_in, weight, preferred_element_type=jnp.float32)

    def slot_update(carry, items):
        down_accumulator, up_accumulator = carry
        x_slot, dy_slot, row_index, col_keep, factor = items
        down_matrix = lax.dynamic_index_in_dim(adapter_down_factor, row_index, 0, keepdims=False)
        up_matrix = lax.dynamic_index_in_dim(adapter_up_factor, row_index, 0, keepdims=False)
        u_full = jnp.dot(x_slot, down_matrix, preferred_element_type=jnp.float32)
        narrow_activation = (u_full * col_keep[None, :]).astype(jnp.bfloat16)
        adapter_output = jnp.dot(narrow_activation, up_matrix, preferred_element_type=jnp.float32)
        g_full = jnp.dot(dy_slot, up_matrix.T, preferred_element_type=jnp.float32)
        narrow_gradient = (g_full * col_keep[None, :] * factor).astype(jnp.bfloat16)
        adapter_backward = jnp.dot(narrow_gradient, down_matrix.T, preferred_element_type=jnp.float32)
        down_accumulator = down_accumulator.at[row_index].add(jnp.dot(x_slot.T, narrow_gradient, preferred_element_type=jnp.float32))
        up_accumulator = up_accumulator.at[row_index].add(factor * jnp.dot(narrow_activation.T, dy_slot, preferred_element_type=jnp.float32))
        return ((down_accumulator, up_accumulator), (adapter_output, adapter_backward))
    empty_down_factor = jnp.zeros((N_DP, MODEL_WIDTH, LARGEST_RANK), jnp.float32)
    empty_up_factor = jnp.zeros((N_DP, LARGEST_RANK, MODEL_WIDTH), jnp.float32)
    (down_accumulator, up_accumulator), (adapter_output, adapter_backward) = lax.scan(slot_update, (empty_down_factor, empty_up_factor), (packed_tokens, masked_values, factor_storage, column_mask, adapter_scale))
    feature_columns = MODEL_WIDTH // N_TENSOR

    def shard_step(running, shard):
        offset = (shard * feature_columns).astype(jnp.int32)
        cols = lax.dynamic_slice_in_dim(flat_dy, offset, feature_columns, 1)
        wcols = lax.dynamic_slice_in_dim(weight, offset, feature_columns, 1)
        partial_sum = jnp.dot(cols, wcols.T, preferred_element_type=jnp.float32)
        rounded = lax.optimization_barrier(partial_sum.astype(jnp.bfloat16)).astype(jnp.float32)
        return (running + rounded, None)
    returned_sum, _ = lax.scan(shard_step, jnp.zeros((slot_count * MICRO_TOKENS, MODEL_WIDTH), jnp.float32), jnp.arange(N_TENSOR, dtype=jnp.int32))
    live_mask3 = live[:, :, None]
    outputs = (live_mask3 * (frozen_output.reshape(slot_count, MICRO_TOKENS, MODEL_WIDTH) + adapter_scale[:, None, None] * adapter_output)).astype(jnp.bfloat16).reshape(-1, MODEL_WIDTH)
    packed_input_gradient = (live_mask3 * (returned_sum.reshape(slot_count, MICRO_TOKENS, MODEL_WIDTH) + adapter_backward)).astype(jnp.bfloat16).reshape(-1, MODEL_WIDTH)
    return (outputs, packed_input_gradient, down_accumulator.astype(jnp.bfloat16), up_accumulator.astype(jnp.bfloat16))
```

```python
import jax
import jax.numpy as jnp
from jax import lax
from jax.sharding import PartitionSpec as P

RANK_LOW = 16
LARGEST_RANK = 256
CAP = 2
MICRO_TOKENS = 16


def swap(value, bit, n):
    return lax.ppermute(value, "dp", [(i, i ^ bit) for i in range(n)])


def offsets_of(n):
    offsets = [0]
    bit = n // 2
    while bit:
        offsets += [o ^ bit for o in offsets]
        bit //= 2
    return offsets


def gather_blocks(value, n):
    blocks = {0: value}
    bit = n // 2
    while bit:
        for o in list(blocks):
            blocks[o ^ bit] = swap(blocks[o], bit, n)
        bit //= 2
    return jnp.concatenate([blocks[o] for o in offsets_of(n)], axis=0)


def reduce_blocks(value, n):
    rows = value.shape[0] // n
    blocks = {o: value[j * rows : (j + 1) * rows] for j, o in enumerate(offsets_of(n))}
    bit = 1
    while bit < n:
        blocks = {o: blocks[o] + swap(blocks[o | bit], bit, n) for o in blocks if not o & bit}
        bit *= 2
    return blocks[0]


def rows_of(values):
    return jnp.repeat(values, MICRO_TOKENS)


def packing(micro_destination_group, micro_adapter, micro_token_count, adapter_home_row, n, me):
    groups = micro_destination_group[:, 0]
    count_all = groups.shape[0]
    per_group = count_all // n
    indices = jnp.arange(count_all, dtype=jnp.int32)
    source = indices // per_group
    earlier = (
        (groups[:, None] == groups[None, :])
        & (source[:, None] == source[None, :])
        & (indices[None, :] < indices[:, None])
    )
    placing = jnp.sum(earlier.astype(jnp.int32), axis=1)
    target = groups * (n * CAP) + source * CAP + placing
    peers = me ^ jnp.array(offsets_of(n), dtype=jnp.int32)
    micro_ids = (
        peers[:, None] * per_group + jnp.arange(per_group, dtype=jnp.int32)[None, :]
    ).reshape(-1)
    slot_ids = (peers[:, None] * (n * CAP) + jnp.arange(n * CAP, dtype=jnp.int32)[None, :]).reshape(
        -1
    )
    here = (micro_ids[:, None] == indices[None, :]).astype(jnp.int32)
    micro_target = jnp.sum(here * target[None, :], axis=1)
    select = (slot_ids[:, None] == target[None, :]).astype(jnp.int32)
    adapter = jnp.sum(select * micro_adapter[None, :], axis=1)
    counted = jnp.sum(select * micro_token_count[None, :], axis=1)
    table_ids = jnp.arange(adapter_home_row.shape[0], dtype=jnp.int32)
    matches = (adapter[:, None] == table_ids[None, :]).astype(jnp.int32)
    home = jnp.sum(matches * adapter_home_row[None, :], axis=1)
    return micro_target, slot_ids, home, counted


def local(
    tokens,
    weight,
    adapter_down_factor,
    adapter_up_factor,
    cotangent,
    micro_destination_group,
    micro_adapter,
    micro_token_count,
    adapter_rank_bucket,
    adapter_home_row,
):
    n = lax.axis_size("dp")
    me = lax.axis_index("dp")
    n_tensor = lax.axis_size("tensor")
    features = tokens.shape[1]
    own_rows = cotangent.shape[0]
    f32, bf16 = jnp.float32, jnp.bfloat16
    down, up = adapter_down_factor[0], adapter_up_factor[0]

    x_all = gather_blocks(tokens, n)
    dy_all = gather_blocks(cotangent, n)

    back_part = lax.dot_general(
        weight, cotangent, (((1,), (1,)), ((), ())), preferred_element_type=f32
    ).astype(bf16)
    back = lax.psum_scatter(back_part, "tensor", scatter_dimension=0, tiled=True).T

    micro_target, slot_ids, home, counted = packing(
        micro_destination_group, micro_adapter, micro_token_count, adapter_home_row, n, me
    )
    token = jnp.arange(x_all.shape[0], dtype=jnp.int32) % MICRO_TOKENS
    place = jnp.arange(dy_all.shape[0], dtype=jnp.int32) % MICRO_TOKENS
    move = (
        (rows_of(slot_ids) * MICRO_TOKENS + place)[:, None]
        == (rows_of(micro_target) * MICRO_TOKENS + token)[None, :]
    ).astype(bf16)
    live = place < rows_of(counted)
    mine = (live & (rows_of(home) == me)).astype(f32)[:, None]
    own_live = live[:own_rows].astype(f32)[:, None]
    bucket = jnp.sum(jnp.where(adapter_home_row == me, adapter_rank_bucket, 0))
    rank = RANK_LOW * jnp.where(bucket == 0, 1, jnp.where(bucket == 1, 4, 16))
    scale = jnp.sqrt(LARGEST_RANK / rank.astype(f32))
    columns = (jnp.arange(LARGEST_RANK, dtype=jnp.int32) < rank).astype(f32)[None, :]

    x_own = jnp.dot(move[:own_rows], x_all, preferred_element_type=f32).astype(bf16)
    x_full = lax.all_gather(x_own, "tensor", axis=1, tiled=True)
    base = jnp.dot(x_full, weight, preferred_element_type=f32)

    u_part = jnp.dot(x_all, down, preferred_element_type=f32).astype(bf16)
    g_part = lax.dot_general(
        dy_all, up, (((1,), (1,)), ((), ())), preferred_element_type=f32
    ).astype(bf16)
    u_sum, g_sum = lax.psum(u_part, "tensor"), lax.psum(g_part, "tensor")

    low_source = (u_sum.astype(f32) * columns).astype(bf16)
    low = (jnp.dot(move, low_source, preferred_element_type=f32) * mine).astype(bf16)
    grad_low = (g_sum.astype(f32) * columns * scale * mine).astype(bf16)
    grad_low_source = lax.dot_general(
        move, grad_low, (((0,), (0,)), ((), ())), preferred_element_type=f32
    ).astype(bf16)

    out_delta = (scale * jnp.dot(low, up, preferred_element_type=f32)).astype(bf16)
    out_delta = reduce_blocks(out_delta, n)
    back_delta = lax.dot_general(
        grad_low, down, (((1,), (1,)), ((), ())), preferred_element_type=f32
    ).astype(bf16)
    back_delta = reduce_blocks(back_delta, n)

    grad_a = lax.dot_general(
        x_all, grad_low_source, (((0,), (0,)), ((), ())), preferred_element_type=f32
    )
    grad_b = scale * lax.dot_general(
        low, dy_all, (((0,), (0,)), ((), ())), preferred_element_type=f32
    )
    outputs = own_live * (base + out_delta.astype(f32))
    input_gradient = own_live * (back.astype(f32) + back_delta.astype(f32))
    return (
        outputs.astype(bf16),
        input_gradient.astype(bf16),
        grad_a.astype(bf16)[None],
        grad_b.astype(bf16)[None],
    )


def solution(mesh):
    in_specs = (
        P(("parts", "dp"), "tensor"),
        P(None, "tensor"),
        P(("parts", "dp"), "tensor", None),
        P(("parts", "dp"), None, "tensor"),
        P(("parts", "dp"), "tensor"),
        P("parts", None),
        P("parts"),
        P("parts"),
        P("parts"),
        P("parts"),
    )
    out_specs = (
        P(("parts", "dp"), "tensor"),
        P(("parts", "dp"), "tensor"),
        P(("parts", "dp"), "tensor", None),
        P(("parts", "dp"), None, "tensor"),
    )
    return jax.shard_map(local, mesh=mesh, in_specs=in_specs, out_specs=out_specs, check_vma=False)
```

```python
import jax
import jax.numpy as jnp
from jax import lax
from jax.experimental import pallas as pl
from jax.experimental.pallas import tpu as pltpu
from jax.sharding import PartitionSpec as P

RANK_LOW = 16
LARGEST_RANK = 256
CAP = 2
MICRO_TOKENS = 16


def swap(value, bit, n):
    return lax.ppermute(value, "dp", [(i, i ^ bit) for i in range(n)])


def offsets_of(n):
    offsets = [0]
    bit = n // 2
    while bit:
        offsets += [o ^ bit for o in offsets]
        bit //= 2
    return offsets


def gather_blocks(value, n):
    blocks = {0: value}
    bit = n // 2
    while bit:
        for o in list(blocks):
            blocks[o ^ bit] = swap(blocks[o], bit, n)
        bit //= 2
    return jnp.concatenate([blocks[o] for o in offsets_of(n)], axis=0)


def reduce_blocks(value, n):
    rows = value.shape[0] // n
    blocks = {o: value[j * rows : (j + 1) * rows] for j, o in enumerate(offsets_of(n))}
    bit = 1
    while bit < n:
        blocks = {o: blocks[o] + swap(blocks[o | bit], bit, n) for o in blocks if not o & bit}
        bit *= 2
    return blocks[0]


def rows_of(values):
    return jnp.repeat(values, MICRO_TOKENS)


def packing(micro_destination_group, micro_adapter, micro_token_count, adapter_home_row, n, me):
    groups = micro_destination_group[:, 0]
    count_all = groups.shape[0]
    per_group = count_all // n
    indices = jnp.arange(count_all, dtype=jnp.int32)
    source = indices // per_group
    earlier = (
        (groups[:, None] == groups[None, :])
        & (source[:, None] == source[None, :])
        & (indices[None, :] < indices[:, None])
    )
    placing = jnp.sum(earlier.astype(jnp.int32), axis=1)
    target = groups * (n * CAP) + source * CAP + placing
    peers = me ^ jnp.array(offsets_of(n), dtype=jnp.int32)
    micro_ids = (
        peers[:, None] * per_group + jnp.arange(per_group, dtype=jnp.int32)[None, :]
    ).reshape(-1)
    slot_ids = (peers[:, None] * (n * CAP) + jnp.arange(n * CAP, dtype=jnp.int32)[None, :]).reshape(
        -1
    )
    here = (micro_ids[:, None] == indices[None, :]).astype(jnp.int32)
    micro_target = jnp.sum(here * target[None, :], axis=1)
    select = (slot_ids[:, None] == target[None, :]).astype(jnp.int32)
    adapter = jnp.sum(select * micro_adapter[None, :], axis=1)
    counted = jnp.sum(select * micro_token_count[None, :], axis=1)
    table_ids = jnp.arange(adapter_home_row.shape[0], dtype=jnp.int32)
    matches = (adapter[:, None] == table_ids[None, :]).astype(jnp.int32)
    home = jnp.sum(matches * adapter_home_row[None, :], axis=1)
    micro_matches = (micro_adapter[:, None] == table_ids[None, :]).astype(jnp.int32)
    micro_home = jnp.sum(micro_matches * adapter_home_row[None, :], axis=1)
    micro_home = jnp.sum(here * micro_home[None, :], axis=1)
    return micro_target, micro_home, slot_ids, home, counted


def layer_kernel(
    tokens, cotangent, weight, down, up, move, micro_mine, mine, own_live, columns, scale,
    outputs, input_gradient, grad_a, grad_b,
    x_all, dy_all, gathered, part, up_got, down_got, up_sum, down_sum, blocks,
    narrow, narrow_pair, narrow_sum, narrow_peer, narrow_own, narrow_got, narrow_all,
    out_delta, out_pair, out_sum, out_peer, back_delta, back_pair, back_sum, back_peer,
    base, load_sem, send_sem, recv_sem,
):
    f32, bf16 = jnp.float32, jnp.bfloat16
    me, spot = lax.axis_index("dp"), lax.axis_index("tensor")
    core_peer = me + 1 - 2 * lax.rem(me, 2)
    chip_peer = lax.rem(me + 2, 4)
    rows, features = tokens.shape
    rank = down.shape[1]
    tile = 256
    low_half = spot < 2
    far_index = jnp.where(low_half, lax.rem(spot + 3, 4), lax.rem(spot + 1, 4))
    middle_index = lax.rem(spot + 2, 4)
    near_index = jnp.where(low_half, spot + 1, spot - 1)
    FAR, MIDDLE, NEAR, OWN = 0, 1, 2, 3
    count = [0]

    def remote(src, dst, target):
        k = count[0]
        count[0] += 1
        return pltpu.make_async_remote_copy(
            src_ref=src, dst_ref=dst, send_sem=send_sem.at[k], recv_sem=recv_sem.at[k],
            device_id=target, device_id_type=pl.DeviceIdType.MESH,
        )

    def load(k, slot, index):
        start = pl.multiple_of(index * features, features)
        return pltpu.make_async_copy(
            weight.at[pl.ds(start, features), :], blocks.at[slot], load_sem.at[k]
        )

    def tiles(size, body):
        @pl.loop(0, size // tile)
        def _(i):
            body(pl.ds(pl.multiple_of(i * tile, tile), tile))

    def nn(a, b):
        return jnp.dot(a, b, preferred_element_type=f32)

    def nt(a, b):
        return lax.dot_general(a, b, (((1,), (1,)), ((), ())), preferred_element_type=f32)

    far_load, middle_load = load(0, 0, far_index), load(1, 1, middle_index)
    near_load, own_load = load(2, 2, near_index), load(3, 0, spot)
    again_load = load(4, 2, far_index)
    for copy in (far_load, middle_load, near_load):
        copy.start()

    barrier = pltpu.get_barrier_semaphore()
    partners = [{"dp": core_peer}, {"dp": chip_peer}]
    partners += [{"tensor": lax.rem(spot + k, 4)} for k in (1, 2, 3)]
    for partner in partners:
        pl.semaphore_signal(barrier, inc=1, device_id=partner, device_id_type=pl.DeviceIdType.MESH)
    pl.semaphore_wait(barrier, len(partners))

    chip, core = {"dp": chip_peer}, {"dp": core_peer}
    above, below = {"tensor": lax.rem(spot + 1, 4)}, {"tensor": lax.rem(spot + 3, 4)}

    def block(ref, j):
        return ref.at[pl.ds(j * rows, rows), :]

    x_chip = remote(tokens, block(x_all, 1), chip)
    x_core = remote(tokens, block(x_all, 2), core)
    x_last = remote(block(x_all, 1), block(x_all, 3), core)
    dy_chip = remote(cotangent, block(dy_all, 1), chip)
    dy_core = remote(cotangent, block(dy_all, 2), core)
    dy_last = remote(block(dy_all, 1), block(dy_all, 3), core)
    x_chip.start()
    x_core.start()
    dy_chip.start()
    dy_core.start()
    x_all[0:rows, :] = tokens[...]
    dy_all[0:rows, :] = cotangent[...]

    def backward(which, slot):
        def body(at):
            part[which, :, at] = nt(cotangent[...], blocks[slot, at, :]).astype(bf16)

        tiles(features, body)

    def forward(index, slot, first=False):
        def body(at):
            term = nn(gathered[index], blocks[slot, :, at])
            base[:, at] = term if first else base[:, at] + term

        tiles(features, body)

    def add(target, a, b):
        def body(at):
            target[:, at] = (a[:, at].astype(f32) + b[:, at].astype(f32)).astype(bf16)

        tiles(target.shape[1], body)

    up_far = remote(part.at[FAR], up_got.at[0], above)
    down_far = remote(part.at[FAR], down_got.at[0], below)
    up_middle = remote(up_sum.at[0], up_got.at[1], above)
    down_middle = remote(down_sum.at[0], down_got.at[1], below)
    up_near = remote(up_sum.at[1], up_got.at[2], above)
    down_near = remote(down_sum.at[1], down_got.at[2], below)
    up_gather = [
        remote(gathered.at[lax.rem(spot + 4 - k, 4)], gathered.at[lax.rem(spot + 4 - k, 4)], above)
        for k in range(3)
    ]
    down_gather = [
        remote(gathered.at[lax.rem(spot + k, 4)], gathered.at[lax.rem(spot + k, 4)], below)
        for k in range(3)
    ]

    far_load.wait()
    backward(FAR, 0)
    pl.when(spot == 0)(up_far.start)
    pl.when(spot == 3)(down_far.start)
    own_load.start()
    x_chip.wait_recv()
    x_last.start()

    middle_load.wait()
    backward(MIDDLE, 1)

    @pl.when(spot == 0)
    def _():
        up_sum[0] = part[MIDDLE]
        up_middle.start()

    @pl.when(spot == 3)
    def _():
        down_sum[0] = part[MIDDLE]
        down_middle.start()

    x_core.wait_recv()
    x_last.wait_recv()

    def pack(at):
        gathered[spot, :, at] = nn(move[0:rows, :], x_all[:, at]).astype(bf16)

    tiles(features, pack)
    pl.when(spot < 3)(up_gather[0].start)
    pl.when(spot > 0)(down_gather[0].start)
    narrow[:, 0:rank] = (nn(x_all[...], down[...]) * micro_mine[...]).astype(bf16)

    near_load.wait()
    backward(NEAR, 2)
    dy_chip.wait_recv()
    dy_last.start()

    @pl.when(spot == 1)
    def _():
        up_far.wait_recv()
        add(up_sum.at[0], part.at[MIDDLE], up_got.at[0])
        up_middle.start()

    @pl.when(spot == 2)
    def _():
        down_far.wait_recv()
        add(down_sum.at[0], part.at[MIDDLE], down_got.at[0])
        down_middle.start()

    dy_core.wait_recv()
    dy_last.wait_recv()
    narrow[:, rank : 2 * rank] = (nt(dy_all[...], up[...]) * mine[...]).astype(bf16)
    pair = remote(narrow.at[pl.ds(2 * rows, 2 * rows), :], narrow_pair, core)
    pair.start()
    own_load.wait()
    backward(OWN, 0)

    @pl.when(spot == 0)
    def _():
        up_sum[1] = part[NEAR]
        up_near.start()

    @pl.when(spot == 3)
    def _():
        down_sum[1] = part[NEAR]
        down_near.start()

    pair.wait_recv()
    narrow_sum[...] = narrow[rows : 2 * rows, :] + narrow_pair[rows : 2 * rows, :]
    peer = remote(narrow_sum, narrow_peer, chip)
    peer.start()
    forward(spot, 0, first=True)

    peer.wait_recv()
    narrow_own[...] = narrow[0:rows, :] + narrow_pair[0:rows, :] + narrow_peer[...]
    spread = [
        remote(narrow_own, narrow_got.at[k - 1], {"tensor": lax.rem(spot + k, 4)})
        for k in (1, 2, 3)
    ]
    for copy in spread:
        copy.start()

    @pl.when((spot == 1) | (spot == 2))
    def _():
        up_middle.wait_recv()
        down_middle.wait_recv()

    @pl.when(spot == 1)
    def _():
        add(up_sum.at[1], part.at[NEAR], up_got.at[1])
        add(down_sum.at[1], part.at[FAR], down_got.at[1])
        up_near.start()
        down_near.start()

    @pl.when(spot == 2)
    def _():
        add(up_sum.at[1], part.at[FAR], up_got.at[1])
        add(down_sum.at[1], part.at[NEAR], down_got.at[1])
        up_near.start()
        down_near.start()

    def pass_on(k):
        @pl.when(spot >= k)
        def _():
            up_gather[k - 1].wait_recv()

        @pl.when(spot <= 3 - k)
        def _():
            down_gather[k - 1].wait_recv()

        if k < 3:
            pl.when((spot >= k) & (spot < 3))(up_gather[k].start)
            pl.when((spot <= 3 - k) & (spot > 0))(down_gather[k].start)

    pass_on(1)
    forward(near_index, 2)
    again_load.start()

    for copy in spread:
        copy.wait_recv()
    total = narrow_own[...].astype(f32)
    for k in range(3):
        total = total + narrow_got[k].astype(f32)
    narrow_all[0:rows, :] = total.astype(bf16)
    all_chip = remote(block(narrow_all, 0), block(narrow_all, 1), chip)
    all_core = remote(block(narrow_all, 0), block(narrow_all, 2), core)
    all_last = remote(block(narrow_all, 1), block(narrow_all, 3), core)
    all_chip.start()
    all_core.start()
    all_chip.wait_recv()
    all_last.start()
    pass_on(2)
    all_core.wait_recv()
    all_last.wait_recv()

    low_source = (narrow_all[:, 0:rank].astype(f32) * columns[...]).astype(bf16)
    low_wide = nn(move[...], low_source) * mine[...]
    low = low_wide.astype(bf16)
    factor = columns[...] * scale[...]
    grad_low_wide = narrow_all[:, rank : 2 * rank].astype(f32) * factor * mine[...]
    grad_low = grad_low_wide.astype(bf16)

    def deltas(at):
        out_delta[:, at] = (scale[...] * nn(low, up[:, at])).astype(bf16)
        back_delta[:, at] = nt(grad_low, down[at, :]).astype(bf16)

    tiles(features, deltas)
    second = pl.ds(2 * rows, 2 * rows)
    out_core = remote(out_delta.at[second, :], out_pair, core)
    back_core = remote(back_delta.at[second, :], back_pair, core)
    out_core.start()
    back_core.start()
    forward(middle_index, 1)
    out_core.wait_recv()
    add(out_sum, block(out_delta, 1), block(out_pair, 1))
    out_chip = remote(out_sum, out_peer, chip)
    out_chip.start()
    back_core.wait_recv()
    add(back_sum, block(back_delta, 1), block(back_pair, 1))
    back_chip = remote(back_sum, back_peer, chip)
    back_chip.start()

    low_turned = low_wide.T.astype(bf16)
    grad_turned = nn(grad_low_wide.T.astype(bf16), move[...]).astype(bf16)

    def gradients(at):
        grad_b[:, at] = (scale[...] * nn(low_turned, dy_all[:, at])).astype(bf16)
        grad_a[at, :] = nn(grad_turned, x_all[:, at]).T.astype(bf16)

    tiles(features, gradients)
    pass_on(3)
    again_load.wait()
    forward(far_index, 2)
    out_chip.wait_recv()

    def finish_out(at):
        delta = out_delta[0:rows, at].astype(f32) + out_pair[0:rows, at].astype(f32)
        delta = delta + out_peer[:, at].astype(f32)
        outputs[:, at] = (own_live[...] * (base[:, at] + delta)).astype(bf16)

    tiles(features, finish_out)
    base[...] = part[OWN].astype(f32)

    @pl.when(spot > 0)
    def _():
        up_near.wait_recv()
        base[...] = base[...] + up_got[2].astype(f32)

    @pl.when(spot < 3)
    def _():
        down_near.wait_recv()
        base[...] = base[...] + down_got[2].astype(f32)

    back_chip.wait_recv()

    def finish_back(at):
        delta = back_delta[0:rows, at].astype(f32) + back_pair[0:rows, at].astype(f32)
        delta = delta + back_peer[:, at].astype(f32)
        input_gradient[:, at] = (own_live[...] * (base[:, at] + delta)).astype(bf16)

    tiles(features, finish_back)

    for copy in (x_chip, x_core, x_last, dy_chip, dy_core, dy_last, pair, peer, *spread):
        copy.wait_send()
    for copy in (all_chip, all_core, all_last, out_core, out_chip, back_core, back_chip):
        copy.wait_send()
    pl.when(spot == 0)(up_far.wait_send)
    pl.when(spot == 3)(down_far.wait_send)
    pl.when(spot < 2)(up_middle.wait_send)
    pl.when(spot >= 2)(down_middle.wait_send)
    pl.when(spot < 3)(up_near.wait_send)
    pl.when(spot > 0)(down_near.wait_send)
    for k in range(3):
        pl.when((spot >= k) & (spot < 3))(up_gather[k].wait_send)
        pl.when((spot <= 3 - k) & (spot > 0))(down_gather[k].wait_send)


def layer(tokens, cotangent, weight, down, up, *rest):
    rows, features = tokens.shape
    rank = down.shape[1]
    bf16 = jnp.bfloat16

    def held(*shape):
        return pltpu.VMEM(shape, bf16)

    vmem = pl.BlockSpec(memory_space=pltpu.VMEM)
    all_rows = 4 * rows
    return pl.pallas_call(
        layer_kernel,
        out_shape=(
            jax.ShapeDtypeStruct((rows, features), bf16),
            jax.ShapeDtypeStruct((rows, features), bf16),
            jax.ShapeDtypeStruct((features, rank), bf16),
            jax.ShapeDtypeStruct((rank, features), bf16),
        ),
        in_specs=[vmem, vmem, pl.BlockSpec(memory_space=pl.ANY)] + [vmem] * (2 + len(rest)),
        out_specs=(vmem,) * 4,
        scratch_shapes=[
            held(all_rows, features),
            held(all_rows, features),
            held(4, rows, features),
            held(4, rows, features),
            held(3, rows, features),
            held(3, rows, features),
            held(2, rows, features),
            held(2, rows, features),
            held(3, features, features),
            held(all_rows, 2 * rank),
            held(2 * rows, 2 * rank),
            held(rows, 2 * rank),
            held(rows, 2 * rank),
            held(rows, 2 * rank),
            held(3, rows, 2 * rank),
            held(all_rows, 2 * rank),
            held(all_rows, features),
            held(2 * rows, features),
            held(rows, features),
            held(rows, features),
            held(all_rows, features),
            held(2 * rows, features),
            held(rows, features),
            held(rows, features),
            pltpu.VMEM((rows, features), jnp.float32),
            pltpu.SemaphoreType.DMA((5,)),
            pltpu.SemaphoreType.DMA((40,)),
            pltpu.SemaphoreType.DMA((40,)),
        ],
        compiler_params=pltpu.CompilerParams(
            collective_id=0, has_side_effects=True, vmem_limit_bytes=60 * 1024 * 1024
        ),
        name="layer",
    )(tokens, cotangent, weight, down, up, *rest)


def local(
    tokens,
    weight,
    adapter_down_factor,
    adapter_up_factor,
    cotangent,
    micro_destination_group,
    micro_adapter,
    micro_token_count,
    adapter_rank_bucket,
    adapter_home_row,
):
    n = lax.axis_size("dp")
    me = lax.axis_index("dp")
    n_tensor = lax.axis_size("tensor")
    features = tokens.shape[1]
    own_rows = cotangent.shape[0]
    f32, bf16 = jnp.float32, jnp.bfloat16
    down, up = adapter_down_factor[0], adapter_up_factor[0]

    micro_target, micro_home, slot_ids, home, counted = packing(
        micro_destination_group, micro_adapter, micro_token_count, adapter_home_row, n, me
    )
    token = jnp.arange(tokens.shape[0] * n, dtype=jnp.int32) % MICRO_TOKENS
    place = jnp.arange(own_rows * n, dtype=jnp.int32) % MICRO_TOKENS
    move = (
        (rows_of(slot_ids) * MICRO_TOKENS + place)[:, None]
        == (rows_of(micro_target) * MICRO_TOKENS + token)[None, :]
    ).astype(bf16)
    live = place < rows_of(counted)
    mine = (live & (rows_of(home) == me)).astype(f32)[:, None]
    micro_mine = (rows_of(micro_home) == me).astype(f32)[:, None]
    own_live = live[:own_rows].astype(f32)[:, None]
    bucket = jnp.sum(jnp.where(adapter_home_row == me, adapter_rank_bucket, 0))
    rank = RANK_LOW * jnp.where(bucket == 0, 1, jnp.where(bucket == 1, 4, 16))
    scale = jnp.sqrt(LARGEST_RANK / rank.astype(f32))
    columns = (jnp.arange(LARGEST_RANK, dtype=jnp.int32) < rank).astype(f32)[None, :]

    if n == 4 and n_tensor == 4 and tokens.shape == cotangent.shape:
        outputs, input_gradient, grad_a, grad_b = layer(
            tokens, cotangent, weight, down, up, move, micro_mine, mine, own_live, columns,
            scale.reshape(1, 1),
        )
        return outputs, input_gradient, grad_a[None], grad_b[None]

    x_all = gather_blocks(tokens, n)
    dy_all = gather_blocks(cotangent, n)

    back_part = lax.dot_general(
        weight, cotangent, (((1,), (1,)), ((), ())), preferred_element_type=f32
    ).astype(bf16)
    back = lax.psum_scatter(back_part, "tensor", scatter_dimension=0, tiled=True).T

    x_own = jnp.dot(move[:own_rows], x_all, preferred_element_type=f32).astype(bf16)
    x_full = lax.all_gather(x_own, "tensor", axis=1, tiled=True)
    base = jnp.dot(x_full, weight, preferred_element_type=f32)

    u_part = jnp.dot(x_all, down, preferred_element_type=f32).astype(bf16)
    g_part = lax.dot_general(
        dy_all, up, (((1,), (1,)), ((), ())), preferred_element_type=f32
    ).astype(bf16)
    u_sum, g_sum = lax.psum(u_part, "tensor"), lax.psum(g_part, "tensor")

    low_source = (u_sum.astype(f32) * columns).astype(bf16)
    low = (jnp.dot(move, low_source, preferred_element_type=f32) * mine).astype(bf16)
    grad_low = (g_sum.astype(f32) * columns * scale * mine).astype(bf16)
    grad_low_source = lax.dot_general(
        move, grad_low, (((0,), (0,)), ((), ())), preferred_element_type=f32
    ).astype(bf16)

    out_delta = (scale * jnp.dot(low, up, preferred_element_type=f32)).astype(bf16)
    out_delta = reduce_blocks(out_delta, n)
    back_delta = lax.dot_general(
        grad_low, down, (((1,), (1,)), ((), ())), preferred_element_type=f32
    ).astype(bf16)
    back_delta = reduce_blocks(back_delta, n)

    grad_a = lax.dot_general(
        x_all, grad_low_source, (((0,), (0,)), ((), ())), preferred_element_type=f32
    )
    grad_b = scale * lax.dot_general(
        low, dy_all, (((0,), (0,)), ((), ())), preferred_element_type=f32
    )
    outputs = own_live * (base + out_delta.astype(f32))
    input_gradient = own_live * (back.astype(f32) + back_delta.astype(f32))
    return (
        outputs.astype(bf16),
        input_gradient.astype(bf16),
        grad_a.astype(bf16)[None],
        grad_b.astype(bf16)[None],
    )


def solution(mesh):
    in_specs = (
        P(("parts", "dp"), "tensor"),
        P(None, "tensor"),
        P(("parts", "dp"), "tensor", None),
        P(("parts", "dp"), None, "tensor"),
        P(("parts", "dp"), "tensor"),
        P("parts", None),
        P("parts"),
        P("parts"),
        P("parts"),
        P("parts"),
    )
    out_specs = (
        P(("parts", "dp"), "tensor"),
        P(("parts", "dp"), "tensor"),
        P(("parts", "dp"), "tensor", None),
        P(("parts", "dp"), None, "tensor"),
    )
    return jax.shard_map(local, mesh=mesh, in_specs=in_specs, out_specs=out_specs, check_vma=False)
```

```python
import functools

import jax
import jax.numpy as jnp
from jax import lax
from jax.experimental import pallas as pl
from jax.experimental.pallas import tpu as pltpu
from jax.sharding import PartitionSpec as P

RANK_LOW = 16
LARGEST_RANK = 256
CAP = 2
MICRO_TOKENS = 16


def swap(value, bit, n):
    return lax.ppermute(value, "dp", [(i, i ^ bit) for i in range(n)])


def offsets_of(n):
    offsets = [0]
    bit = n // 2
    while bit:
        offsets += [o ^ bit for o in offsets]
        bit //= 2
    return offsets


def gather_blocks(value, n):
    blocks = {0: value}
    bit = n // 2
    while bit:
        for o in list(blocks):
            blocks[o ^ bit] = swap(blocks[o], bit, n)
        bit //= 2
    return jnp.concatenate([blocks[o] for o in offsets_of(n)], axis=0)


def reduce_blocks(value, n):
    rows = value.shape[0] // n
    blocks = {o: value[j * rows : (j + 1) * rows] for j, o in enumerate(offsets_of(n))}
    bit = 1
    while bit < n:
        blocks = {o: blocks[o] + swap(blocks[o | bit], bit, n) for o in blocks if not o & bit}
        bit *= 2
    return blocks[0]


def rows_of(values):
    return jnp.repeat(values, MICRO_TOKENS)


def packing(micro_destination_group, micro_adapter, micro_token_count, adapter_home_row, n, me):
    groups = micro_destination_group[:, 0]
    count_all = groups.shape[0]
    per_group = count_all // n
    indices = jnp.arange(count_all, dtype=jnp.int32)
    source = indices // per_group
    earlier = (
        (groups[:, None] == groups[None, :])
        & (source[:, None] == source[None, :])
        & (indices[None, :] < indices[:, None])
    )
    placing = jnp.sum(earlier.astype(jnp.int32), axis=1)
    target = groups * (n * CAP) + source * CAP + placing
    peers = me ^ jnp.array(offsets_of(n), dtype=jnp.int32)
    micro_ids = (
        peers[:, None] * per_group + jnp.arange(per_group, dtype=jnp.int32)[None, :]
    ).reshape(-1)
    slot_ids = (peers[:, None] * (n * CAP) + jnp.arange(n * CAP, dtype=jnp.int32)[None, :]).reshape(
        -1
    )
    here = (micro_ids[:, None] == indices[None, :]).astype(jnp.int32)
    micro_target = jnp.sum(here * target[None, :], axis=1)
    select = (slot_ids[:, None] == target[None, :]).astype(jnp.int32)
    adapter = jnp.sum(select * micro_adapter[None, :], axis=1)
    counted = jnp.sum(select * micro_token_count[None, :], axis=1)
    table_ids = jnp.arange(adapter_home_row.shape[0], dtype=jnp.int32)
    matches = (adapter[:, None] == table_ids[None, :]).astype(jnp.int32)
    home = jnp.sum(matches * adapter_home_row[None, :], axis=1)
    micro_matches = (micro_adapter[:, None] == table_ids[None, :]).astype(jnp.int32)
    micro_home = jnp.sum(micro_matches * adapter_home_row[None, :], axis=1)
    micro_home = jnp.sum(here * micro_home[None, :], axis=1)
    return micro_target, micro_home, slot_ids, home, counted


def layer_kernel(
    tokens, cotangent, weight, down, up, destination, adapter, live_count, bucket, home_row,
    outputs, input_gradient, grad_a, grad_b,
    x_all, dy_all, gathered, part, up_got, down_got, up_sum, down_sum, blocks,
    move, narrow, narrow_pair, narrow_sum, narrow_peer, narrow_own, narrow_got, narrow_all,
    out_delta, out_pair, out_sum, out_peer, back_delta, back_pair, back_sum, back_peer,
    base, load_sem, send_sem, recv_sem,
):
    f32, bf16 = jnp.float32, jnp.bfloat16
    me, spot = lax.axis_index("dp"), lax.axis_index("tensor")
    core_peer = me + 1 - 2 * lax.rem(me, 2)
    chip_peer = lax.rem(me + 2, 4)
    rows, features = tokens.shape
    rank = down.shape[1]
    tile = 256
    low_half = spot < 2
    far_index = jnp.where(low_half, lax.rem(spot + 3, 4), lax.rem(spot + 1, 4))
    middle_index = lax.rem(spot + 2, 4)
    near_index = jnp.where(low_half, spot + 1, spot - 1)
    FAR, MIDDLE, NEAR, OWN = 0, 1, 2, 3
    count = [0]

    def remote(src, dst, target):
        k = count[0]
        count[0] += 1
        return pltpu.make_async_remote_copy(
            src_ref=src, dst_ref=dst, send_sem=send_sem.at[k], recv_sem=recv_sem.at[k],
            device_id=target, device_id_type=pl.DeviceIdType.MESH,
        )

    def load(k, slot, index):
        start = pl.multiple_of(index * features, features)
        return pltpu.make_async_copy(
            weight.at[pl.ds(start, features), :], blocks.at[slot], load_sem.at[k]
        )

    def tiles(size, body):
        @pl.loop(0, size // tile)
        def _(i):
            body(pl.ds(pl.multiple_of(i * tile, tile), tile))

    def nn(a, b):
        return jnp.dot(a, b, preferred_element_type=f32)

    def nt(a, b):
        return lax.dot_general(a, b, (((1,), (1,)), ((), ())), preferred_element_type=f32)

    far_load, middle_load = load(0, 0, far_index), load(1, 1, middle_index)
    near_load, own_load = load(2, 2, near_index), load(3, 0, spot)
    again_load = load(4, 2, far_index)
    for copy in (far_load, middle_load, near_load):
        copy.start()

    barrier = pltpu.get_barrier_semaphore()
    partners = [{"dp": core_peer}, {"dp": chip_peer}]
    partners += [{"tensor": lax.rem(spot + k, 4)} for k in (1, 2, 3)]
    for partner in partners:
        pl.semaphore_signal(barrier, inc=1, device_id=partner, device_id_type=pl.DeviceIdType.MESH)
    pl.semaphore_wait(barrier, len(partners))

    chip, core = {"dp": chip_peer}, {"dp": core_peer}
    above, below = {"tensor": lax.rem(spot + 1, 4)}, {"tensor": lax.rem(spot + 3, 4)}

    def block(ref, j):
        return ref.at[pl.ds(j * rows, rows), :]

    x_chip = remote(tokens, block(x_all, 1), chip)
    x_core = remote(tokens, block(x_all, 2), core)
    x_last = remote(block(x_all, 1), block(x_all, 3), core)
    dy_chip = remote(cotangent, block(dy_all, 1), chip)
    dy_core = remote(cotangent, block(dy_all, 2), core)
    dy_last = remote(block(dy_all, 1), block(dy_all, 3), core)
    x_chip.start()
    x_core.start()
    dy_core.start()
    x_all[0:rows, :] = tokens[...]
    dy_all[0:rows, :] = cotangent[...]

    def backward(which, slot):
        def body(at):
            part[which, :, at] = nt(cotangent[...], blocks[slot, at, :]).astype(bf16)

        tiles(features, body)

    def forward(index, slot, first=False):
        def body(at):
            term = nn(gathered[index], blocks[slot, :, at])
            base[:, at] = term if first else base[:, at] + term

        tiles(features, body)

    def add(target, a, b):
        def body(at):
            target[:, at] = (a[:, at].astype(f32) + b[:, at].astype(f32)).astype(bf16)

        tiles(target.shape[1], body)

    up_far = remote(part.at[FAR], up_got.at[0], above)
    down_far = remote(part.at[FAR], down_got.at[0], below)
    up_middle = remote(up_sum.at[0], up_got.at[1], above)
    down_middle = remote(down_sum.at[0], down_got.at[1], below)
    up_near = remote(up_sum.at[1], up_got.at[2], above)
    down_near = remote(down_sum.at[1], down_got.at[2], below)
    up_gather = [
        remote(gathered.at[lax.rem(spot + 4 - k, 4)], gathered.at[lax.rem(spot + 4 - k, 4)], above)
        for k in range(3)
    ]
    down_gather = [
        remote(gathered.at[lax.rem(spot + k, 4)], gathered.at[lax.rem(spot + k, 4)], below)
        for k in range(3)
    ]

    def exchange(kind):
        sides = narrow.at[kind], narrow_pair.at[kind], narrow_all.at[kind]
        pair = remote(sides[0].at[pl.ds(2 * rows, 2 * rows), :], sides[1], core)
        peer = remote(narrow_sum.at[kind], narrow_peer.at[kind], chip)
        spread = [
            remote(narrow_own.at[kind], narrow_got.at[kind, k - 1], {"tensor": lax.rem(spot + k, 4)})
            for k in (1, 2, 3)
        ]
        all_chip = remote(block(sides[2], 0), block(sides[2], 1), chip)
        all_core = remote(block(sides[2], 0), block(sides[2], 2), core)
        all_last = remote(block(sides[2], 1), block(sides[2], 3), core)
        return pair, peer, spread, all_chip, all_core, all_last

    def send_peer(kind, steps):
        pair, peer = steps[:2]
        pair.wait_recv()
        narrow_sum[kind] = narrow[kind, rows : 2 * rows, :] + narrow_pair[kind, rows : 2 * rows, :]
        peer.start()

    def send_spread(kind, steps):
        peer, spread = steps[1:3]
        peer.wait_recv()
        narrow_own[kind] = (
            narrow[kind, 0:rows, :] + narrow_pair[kind, 0:rows, :] + narrow_peer[kind]
        )
        for copy in spread:
            copy.start()

    def send_total(kind, steps):
        _, _, spread, all_chip, all_core, _ = steps
        for copy in spread:
            copy.wait_recv()
        total = narrow_own[kind].astype(f32)
        for k in range(3):
            total = total + narrow_got[kind, k].astype(f32)
        narrow_all[kind, 0:rows, :] = total.astype(bf16)
        all_chip.start()
        all_core.start()

    def send_last(steps):
        steps[3].wait_recv()
        steps[5].start()

    def wait_all(steps):
        steps[4].wait_recv()
        steps[5].wait_recv()

    def pass_on(k):
        @pl.when(spot >= k)
        def _():
            up_gather[k - 1].wait_recv()

        @pl.when(spot <= 3 - k)
        def _():
            down_gather[k - 1].wait_recv()

        if k < 3:
            pl.when((spot >= k) & (spot < 3))(up_gather[k].start)
            pl.when((spot <= 3 - k) & (spot > 0))(down_gather[k].start)

    u_steps, g_steps = exchange(0), exchange(1)
    second = pl.ds(2 * rows, 2 * rows)
    out_core = remote(out_delta.at[second, :], out_pair, core)
    back_core = remote(back_delta.at[second, :], back_pair, core)
    out_chip = remote(out_sum, out_peer, chip)
    back_chip = remote(back_sum, back_peer, chip)

    far_load.wait()
    backward(FAR, 0)
    pl.when(spot == 0)(up_far.start)
    pl.when(spot == 3)(down_far.start)
    own_load.start()

    def iota(shape, axis):
        return lax.broadcasted_iota(jnp.int32, shape, axis)

    def total_of(mask, values, axis):
        return jnp.sum(jnp.where(mask, values, 0.0), axis=axis, keepdims=True)

    micros = destination.shape[0]
    per_group = micros // 4
    width = 4 * rows
    first, later = iota((micros, micros), 0), iota((micros, micros), 1)
    to_column = destination[...].astype(f32)
    to_row = total_of(first == later, to_column, 0)
    shares = (first // per_group == later // per_group) & (to_column == to_row)
    place_column = total_of(shares & (later < first), 1.0, 1)
    place_row = total_of(shares & (first < later), 1.0, 0)
    source_column = (iota((micros, 1), 0) // per_group * CAP).astype(f32)
    source_row = (iota((1, micros), 1) // per_group * CAP).astype(f32)
    target_column = to_column * (4.0 * CAP) + source_column + place_column
    target_row = to_row * (4.0 * CAP) + source_row + place_row
    last_peer = lax.rem(core_peer + 2, 4)

    def unit(index):
        j = index // rows
        peer = jnp.where(
            j == 0, me, jnp.where(j == 1, chip_peer, jnp.where(j == 2, core_peer, last_peer))
        )
        return peer * (rows // MICRO_TOKENS) + lax.rem(index, rows) // MICRO_TOKENS

    row_ids, column_ids = iota((width, 1), 0), iota((1, width), 1)
    row_unit, column_unit = unit(row_ids), unit(column_ids)
    row_place, column_place = lax.rem(row_ids, MICRO_TOKENS), lax.rem(column_ids, MICRO_TOKENS)
    column_target = total_of(iota((micros, width), 0) == column_unit, target_column, 0)
    move[...] = jnp.where(
        (row_unit.astype(f32) == column_target) & (row_place == column_place), 1.0, 0.0
    ).astype(bf16)
    home_micro = jnp.zeros((1, micros), f32)
    own_bucket = jnp.int32(0)
    for a in range(home_row.shape[0]):
        home_micro = home_micro + jnp.where(adapter[...] == a, home_row[a].astype(f32), 0.0)
        own_bucket = own_bucket + jnp.where(home_row[a] == me, bucket[a], 0)
    chosen = row_unit.astype(f32) == target_row
    counted = total_of(chosen, live_count[...].astype(f32), 1)
    live = row_place.astype(f32) < counted
    home_here = total_of(chosen, home_micro, 1)
    self_id = me.astype(f32)
    mine = jnp.where(live & (home_here == self_id), 1.0, 0.0)
    own_live = jnp.where(live, 1.0, 0.0)[0:rows, :]
    micro_home = total_of(iota((width, micros), 1) == row_unit, home_micro, 1)
    micro_mine = jnp.where(micro_home == self_id, 1.0, 0.0)
    kept = RANK_LOW * jnp.where(own_bucket == 0, 1, jnp.where(own_bucket == 1, 4, 16))
    columns = jnp.where(iota((1, rank), 1) < kept, 1.0, 0.0)
    scale = jnp.where(own_bucket == 0, 4.0, jnp.where(own_bucket == 1, 2.0, 1.0))

    middle_load.wait()
    backward(MIDDLE, 1)
    near_load.wait()
    backward(NEAR, 2)
    x_chip.wait_recv()
    x_last.start()
    dy_chip.start()
    x_core.wait_recv()
    x_last.wait_recv()

    def pack(at):
        gathered[spot, :, at] = nn(move[0:rows, :], x_all[:, at]).astype(bf16)

    tiles(features, pack)
    pl.when(spot < 3)(up_gather[0].start)
    pl.when(spot > 0)(down_gather[0].start)
    narrow[0] = (nn(x_all[...], down[...]) * micro_mine).astype(bf16)
    u_steps[0].start()
    send_peer(0, u_steps)
    own_load.wait()
    backward(OWN, 0)
    send_spread(0, u_steps)
    forward(spot, 0, first=True)
    dy_chip.wait_recv()
    dy_last.start()
    dy_core.wait_recv()
    dy_last.wait_recv()
    narrow[1] = (nt(dy_all[...], up[...]) * mine).astype(bf16)
    g_steps[0].start()
    pass_on(1)

    @pl.when(spot == 0)
    def _():
        up_sum[0] = part[MIDDLE]
        up_middle.start()

    @pl.when(spot == 3)
    def _():
        down_sum[0] = part[MIDDLE]
        down_middle.start()

    send_peer(1, g_steps)
    send_total(0, u_steps)
    send_spread(1, g_steps)
    send_last(u_steps)
    forward(near_index, 2)
    again_load.start()
    wait_all(u_steps)
    low_source = (narrow_all[0].astype(f32) * columns).astype(bf16)
    low_wide = nn(move[...], low_source) * mine
    low = low_wide.astype(bf16)

    def out_part(at):
        out_delta[:, at] = (scale * nn(low, up[:, at])).astype(bf16)

    tiles(features, out_part)
    out_core.start()
    out_core.wait_recv()
    add(out_sum, block(out_delta, 1), block(out_pair, 1))
    out_chip.start()
    pass_on(2)

    @pl.when(spot == 1)
    def _():
        up_far.wait_recv()
        add(up_sum.at[0], part.at[MIDDLE], up_got.at[0])
        up_middle.start()

    @pl.when(spot == 2)
    def _():
        down_far.wait_recv()
        add(down_sum.at[0], part.at[MIDDLE], down_got.at[0])
        down_middle.start()

    @pl.when(spot == 0)
    def _():
        up_sum[1] = part[NEAR]
        up_near.start()

    @pl.when(spot == 3)
    def _():
        down_sum[1] = part[NEAR]
        down_near.start()

    send_total(1, g_steps)
    send_last(g_steps)
    wait_all(g_steps)
    grad_low_wide = narrow_all[1].astype(f32) * (columns * scale) * mine
    grad_low = grad_low_wide.astype(bf16)

    def back_part(at):
        back_delta[:, at] = nt(grad_low, down[at, :]).astype(bf16)

    tiles(features, back_part)
    back_core.start()
    forward(middle_index, 1)
    back_core.wait_recv()
    add(back_sum, block(back_delta, 1), block(back_pair, 1))
    back_chip.start()

    @pl.when(spot == 1)
    def _():
        up_middle.wait_recv()
        add(up_sum.at[1], part.at[NEAR], up_got.at[1])
        up_near.start()
        down_middle.wait_recv()
        add(down_sum.at[1], part.at[FAR], down_got.at[1])
        down_near.start()

    @pl.when(spot == 2)
    def _():
        down_middle.wait_recv()
        add(down_sum.at[1], part.at[NEAR], down_got.at[1])
        down_near.start()
        up_middle.wait_recv()
        add(up_sum.at[1], part.at[FAR], up_got.at[1])
        up_near.start()

    low_turned = low_wide.T.astype(bf16)
    grad_turned = nn(grad_low_wide.T.astype(bf16), move[...]).astype(bf16)

    def gradients(at):
        grad_b[:, at] = (scale * nn(low_turned, dy_all[:, at])).astype(bf16)
        grad_a[at, :] = nn(grad_turned, x_all[:, at]).T.astype(bf16)

    tiles(features, gradients)
    pass_on(3)
    again_load.wait()
    forward(far_index, 2)
    out_chip.wait_recv()

    def finish_out(at):
        delta = out_delta[0:rows, at].astype(f32) + out_pair[0:rows, at].astype(f32)
        delta = delta + out_peer[:, at].astype(f32)
        outputs[:, at] = (own_live * (base[:, at] + delta)).astype(bf16)

    tiles(features, finish_out)
    base[...] = part[OWN].astype(f32)

    @pl.when(spot > 0)
    def _():
        up_near.wait_recv()
        base[...] = base[...] + up_got[2].astype(f32)

    @pl.when(spot < 3)
    def _():
        down_near.wait_recv()
        base[...] = base[...] + down_got[2].astype(f32)

    back_chip.wait_recv()

    def finish_back(at):
        delta = back_delta[0:rows, at].astype(f32) + back_pair[0:rows, at].astype(f32)
        delta = delta + back_peer[:, at].astype(f32)
        input_gradient[:, at] = (own_live * (base[:, at] + delta)).astype(bf16)

    tiles(features, finish_back)

    for copy in (x_chip, x_core, x_last, dy_chip, dy_core, dy_last):
        copy.wait_send()
    for pair, peer, spread, *rest in (u_steps, g_steps):
        for copy in (pair, peer, *spread, *rest):
            copy.wait_send()
    for copy in (out_core, out_chip, back_core, back_chip):
        copy.wait_send()
    pl.when(spot == 0)(up_far.wait_send)
    pl.when(spot == 3)(down_far.wait_send)
    pl.when(spot < 2)(up_middle.wait_send)
    pl.when(spot >= 2)(down_middle.wait_send)
    pl.when(spot < 3)(up_near.wait_send)
    pl.when(spot > 0)(down_near.wait_send)
    for k in range(3):
        pl.when((spot >= k) & (spot < 3))(up_gather[k].wait_send)
        pl.when((spot <= 3 - k) & (spot > 0))(down_gather[k].wait_send)


def layer(tokens, cotangent, weight, down, up, *rest):
    rows, features = tokens.shape
    rank = down.shape[1]
    bf16 = jnp.bfloat16

    def held(*shape):
        return pltpu.VMEM(shape, bf16)

    vmem = pl.BlockSpec(memory_space=pltpu.VMEM)
    smem = pl.BlockSpec(memory_space=pltpu.SMEM)
    all_rows = 4 * rows
    return pl.pallas_call(
        layer_kernel,
        out_shape=(
            jax.ShapeDtypeStruct((rows, features), bf16),
            jax.ShapeDtypeStruct((rows, features), bf16),
            jax.ShapeDtypeStruct((features, rank), bf16),
            jax.ShapeDtypeStruct((rank, features), bf16),
        ),
        in_specs=[vmem, vmem, pl.BlockSpec(memory_space=pl.ANY)] + [vmem] * 5 + [smem] * 2,
        out_specs=(vmem,) * 4,
        scratch_shapes=[
            held(all_rows, features),
            held(all_rows, features),
            held(4, rows, features),
            held(4, rows, features),
            held(3, rows, features),
            held(3, rows, features),
            held(2, rows, features),
            held(2, rows, features),
            held(3, features, features),
            held(all_rows, all_rows),
            held(2, all_rows, rank),
            held(2, 2 * rows, rank),
            held(2, rows, rank),
            held(2, rows, rank),
            held(2, rows, rank),
            held(2, 3, rows, rank),
            held(2, all_rows, rank),
            held(all_rows, features),
            held(2 * rows, features),
            held(rows, features),
            held(rows, features),
            held(all_rows, features),
            held(2 * rows, features),
            held(rows, features),
            held(rows, features),
            pltpu.VMEM((rows, features), jnp.float32),
            pltpu.SemaphoreType.DMA((5,)),
            pltpu.SemaphoreType.DMA((48,)),
            pltpu.SemaphoreType.DMA((48,)),
        ],
        compiler_params=pltpu.CompilerParams(
            collective_id=0, has_side_effects=True, vmem_limit_bytes=60 * 1024 * 1024
        ),
        name="layer",
    )(tokens, cotangent, weight, down, up, *rest)


def hand_on_kernel(count, *refs):
    sources, results = refs[:count], refs[count : 2 * count]
    held, sems = refs[2 * count : 3 * count], refs[3 * count]
    loads = [
        pltpu.make_async_copy(sources[i], held[i], sems.at[2 * i]) for i in range(count)
    ]
    stores = [
        pltpu.make_async_copy(held[i], results[i], sems.at[2 * i + 1]) for i in range(count)
    ]
    for copy in loads:
        copy.start()
    for load, store in zip(loads, stores):
        load.wait()
        store.start()
    for copy in stores:
        copy.wait()


def handed_on(*arrays):
    anywhere = pl.BlockSpec(memory_space=pltpu.HBM)
    count = len(arrays)
    return pl.pallas_call(
        functools.partial(hand_on_kernel, count),
        out_shape=tuple(jax.ShapeDtypeStruct(a.shape, a.dtype) for a in arrays),
        in_specs=[anywhere] * count,
        out_specs=(anywhere,) * count,
        scratch_shapes=[pltpu.VMEM(a.shape, a.dtype) for a in arrays]
        + [pltpu.SemaphoreType.DMA((2 * count,))],
        compiler_params=pltpu.CompilerParams(vmem_limit_bytes=32 * 1024 * 1024),
        name="hand_on",
    )(*arrays)


def local(
    tokens,
    weight,
    adapter_down_factor,
    adapter_up_factor,
    cotangent,
    micro_destination_group,
    micro_adapter,
    micro_token_count,
    adapter_rank_bucket,
    adapter_home_row,
):
    n = lax.axis_size("dp")
    me = lax.axis_index("dp")
    n_tensor = lax.axis_size("tensor")
    features = tokens.shape[1]
    own_rows = cotangent.shape[0]
    f32, bf16 = jnp.float32, jnp.bfloat16
    down, up = adapter_down_factor[0], adapter_up_factor[0]
    if n == 4 and n_tensor == 4 and tokens.shape == cotangent.shape:
        outputs, input_gradient, grad_a, grad_b = handed_on(
            *layer(
                tokens, cotangent, weight, down, up, micro_destination_group,
                micro_adapter.reshape(1, -1), micro_token_count.reshape(1, -1),
                adapter_rank_bucket, adapter_home_row,
            )
        )
        return outputs, input_gradient, grad_a[None], grad_b[None]

    micro_target, micro_home, slot_ids, home, counted = packing(
        micro_destination_group, micro_adapter, micro_token_count, adapter_home_row, n, me
    )
    token = jnp.arange(tokens.shape[0] * n, dtype=jnp.int32) % MICRO_TOKENS
    place = jnp.arange(own_rows * n, dtype=jnp.int32) % MICRO_TOKENS
    move = (
        (rows_of(slot_ids) * MICRO_TOKENS + place)[:, None]
        == (rows_of(micro_target) * MICRO_TOKENS + token)[None, :]
    ).astype(bf16)
    live = place < rows_of(counted)
    mine = (live & (rows_of(home) == me)).astype(f32)[:, None]
    micro_mine = (rows_of(micro_home) == me).astype(f32)[:, None]
    own_live = live[:own_rows].astype(f32)[:, None]
    bucket = jnp.sum(jnp.where(adapter_home_row == me, adapter_rank_bucket, 0))
    rank = RANK_LOW * jnp.where(bucket == 0, 1, jnp.where(bucket == 1, 4, 16))
    scale = jnp.sqrt(LARGEST_RANK / rank.astype(f32))
    columns = (jnp.arange(LARGEST_RANK, dtype=jnp.int32) < rank).astype(f32)[None, :]

    x_all = gather_blocks(tokens, n)
    dy_all = gather_blocks(cotangent, n)

    back_part = lax.dot_general(
        weight, cotangent, (((1,), (1,)), ((), ())), preferred_element_type=f32
    ).astype(bf16)
    back = lax.psum_scatter(back_part, "tensor", scatter_dimension=0, tiled=True).T

    x_own = jnp.dot(move[:own_rows], x_all, preferred_element_type=f32).astype(bf16)
    x_full = lax.all_gather(x_own, "tensor", axis=1, tiled=True)
    base = jnp.dot(x_full, weight, preferred_element_type=f32)

    u_part = jnp.dot(x_all, down, preferred_element_type=f32).astype(bf16)
    g_part = lax.dot_general(
        dy_all, up, (((1,), (1,)), ((), ())), preferred_element_type=f32
    ).astype(bf16)
    u_sum, g_sum = lax.psum(u_part, "tensor"), lax.psum(g_part, "tensor")

    low_source = (u_sum.astype(f32) * columns).astype(bf16)
    low = (jnp.dot(move, low_source, preferred_element_type=f32) * mine).astype(bf16)
    grad_low = (g_sum.astype(f32) * columns * scale * mine).astype(bf16)
    grad_low_source = lax.dot_general(
        move, grad_low, (((0,), (0,)), ((), ())), preferred_element_type=f32
    ).astype(bf16)

    out_delta = (scale * jnp.dot(low, up, preferred_element_type=f32)).astype(bf16)
    out_delta = reduce_blocks(out_delta, n)
    back_delta = lax.dot_general(
        grad_low, down, (((1,), (1,)), ((), ())), preferred_element_type=f32
    ).astype(bf16)
    back_delta = reduce_blocks(back_delta, n)

    grad_a = lax.dot_general(
        x_all, grad_low_source, (((0,), (0,)), ((), ())), preferred_element_type=f32
    )
    grad_b = scale * lax.dot_general(
        low, dy_all, (((0,), (0,)), ((), ())), preferred_element_type=f32
    )
    outputs = own_live * (base + out_delta.astype(f32))
    input_gradient = own_live * (back.astype(f32) + back_delta.astype(f32))
    return (
        outputs.astype(bf16),
        input_gradient.astype(bf16),
        grad_a.astype(bf16)[None],
        grad_b.astype(bf16)[None],
    )


def solution(mesh):
    in_specs = (
        P(("parts", "dp"), "tensor"),
        P(None, "tensor"),
        P(("parts", "dp"), "tensor", None),
        P(("parts", "dp"), None, "tensor"),
        P(("parts", "dp"), "tensor"),
        P("parts", None),
        P("parts"),
        P("parts"),
        P("parts"),
        P("parts"),
    )
    out_specs = (
        P(("parts", "dp"), "tensor"),
        P(("parts", "dp"), "tensor"),
        P(("parts", "dp"), "tensor", None),
        P(("parts", "dp"), None, "tensor"),
    )
    return jax.shard_map(local, mesh=mesh, in_specs=in_specs, out_specs=out_specs, check_vma=False)
```

```python
import functools

import jax
import jax.numpy as jnp
from jax import lax
from jax.experimental import pallas as pl
from jax.experimental.pallas import tpu as pltpu
from jax.sharding import PartitionSpec as P

RANK_LOW = 16
LARGEST_RANK = 256
CAP = 2
MICRO_TOKENS = 16


def swap(value, bit, n):
    return lax.ppermute(value, "dp", [(i, i ^ bit) for i in range(n)])


def offsets_of(n):
    offsets = [0]
    bit = n // 2
    while bit:
        offsets += [o ^ bit for o in offsets]
        bit //= 2
    return offsets


def gather_blocks(value, n):
    blocks = {0: value}
    bit = n // 2
    while bit:
        for o in list(blocks):
            blocks[o ^ bit] = swap(blocks[o], bit, n)
        bit //= 2
    return jnp.concatenate([blocks[o] for o in offsets_of(n)], axis=0)


def reduce_blocks(value, n):
    rows = value.shape[0] // n
    blocks = {o: value[j * rows : (j + 1) * rows] for j, o in enumerate(offsets_of(n))}
    bit = 1
    while bit < n:
        blocks = {o: blocks[o] + swap(blocks[o | bit], bit, n) for o in blocks if not o & bit}
        bit *= 2
    return blocks[0]


def rows_of(values):
    return jnp.repeat(values, MICRO_TOKENS)


def packing(micro_destination_group, micro_adapter, micro_token_count, adapter_home_row, n, me):
    groups = micro_destination_group[:, 0]
    count_all = groups.shape[0]
    per_group = count_all // n
    indices = jnp.arange(count_all, dtype=jnp.int32)
    source = indices // per_group
    earlier = (
        (groups[:, None] == groups[None, :])
        & (source[:, None] == source[None, :])
        & (indices[None, :] < indices[:, None])
    )
    placing = jnp.sum(earlier.astype(jnp.int32), axis=1)
    target = groups * (n * CAP) + source * CAP + placing
    peers = me ^ jnp.array(offsets_of(n), dtype=jnp.int32)
    micro_ids = (
        peers[:, None] * per_group + jnp.arange(per_group, dtype=jnp.int32)[None, :]
    ).reshape(-1)
    slot_ids = (peers[:, None] * (n * CAP) + jnp.arange(n * CAP, dtype=jnp.int32)[None, :]).reshape(
        -1
    )
    here = (micro_ids[:, None] == indices[None, :]).astype(jnp.int32)
    micro_target = jnp.sum(here * target[None, :], axis=1)
    select = (slot_ids[:, None] == target[None, :]).astype(jnp.int32)
    adapter = jnp.sum(select * micro_adapter[None, :], axis=1)
    counted = jnp.sum(select * micro_token_count[None, :], axis=1)
    table_ids = jnp.arange(adapter_home_row.shape[0], dtype=jnp.int32)
    matches = (adapter[:, None] == table_ids[None, :]).astype(jnp.int32)
    home = jnp.sum(matches * adapter_home_row[None, :], axis=1)
    micro_matches = (micro_adapter[:, None] == table_ids[None, :]).astype(jnp.int32)
    micro_home = jnp.sum(micro_matches * adapter_home_row[None, :], axis=1)
    micro_home = jnp.sum(here * micro_home[None, :], axis=1)
    return micro_target, micro_home, slot_ids, home, counted


def layer_kernel(
    tokens, cotangent, weight, down, up, destination, adapter, live_count, bucket, home_row,
    outputs, input_gradient, grad_a, grad_b,
    x_all, dy_all, gathered, part, up_got, down_got, up_sum, down_sum, blocks,
    move, narrow, narrow_pair, narrow_sum, narrow_peer, narrow_own, narrow_got, narrow_all,
    out_delta, out_pair, out_sum, out_peer, back_delta, back_pair, back_sum, back_peer,
    base, load_sem, send_sem, recv_sem,
):
    f32, bf16 = jnp.float32, jnp.bfloat16
    me, spot = lax.axis_index("dp"), lax.axis_index("tensor")
    core_peer = me + 1 - 2 * lax.rem(me, 2)
    chip_peer = lax.rem(me + 2, 4)
    rows, features = tokens.shape
    rank = down.shape[1]
    tile = 256
    low_half = spot < 2
    far_index = jnp.where(low_half, lax.rem(spot + 3, 4), lax.rem(spot + 1, 4))
    middle_index = lax.rem(spot + 2, 4)
    near_index = jnp.where(low_half, spot + 1, spot - 1)
    FAR, MIDDLE, NEAR, OWN = 0, 1, 2, 3
    count = [0]

    def remote(src, dst, target):
        k = count[0]
        count[0] += 1
        return pltpu.make_async_remote_copy(
            src_ref=src, dst_ref=dst, send_sem=send_sem.at[k], recv_sem=recv_sem.at[k],
            device_id=target, device_id_type=pl.DeviceIdType.MESH,
        )

    def load(k, slot, index):
        start = pl.multiple_of(index * features, features)
        return pltpu.make_async_copy(
            weight.at[pl.ds(start, features), :], blocks.at[slot], load_sem.at[k]
        )

    def tiles(size, body):
        @pl.loop(0, size // tile)
        def _(i):
            body(pl.ds(pl.multiple_of(i * tile, tile), tile))

    def nn(a, b):
        return jnp.dot(a, b, preferred_element_type=f32)

    def nt(a, b):
        return lax.dot_general(a, b, (((1,), (1,)), ((), ())), preferred_element_type=f32)

    far_load, middle_load = load(0, 0, far_index), load(1, 1, middle_index)
    near_load, own_load = load(2, 2, near_index), load(3, 0, spot)
    again_load = load(4, 2, far_index)
    for copy in (far_load, middle_load, near_load):
        copy.start()

    barrier = pltpu.get_barrier_semaphore()
    partners = [{"dp": core_peer}, {"dp": chip_peer}]
    partners += [{"tensor": lax.rem(spot + k, 4)} for k in (1, 2, 3)]
    for partner in partners:
        pl.semaphore_signal(barrier, inc=1, device_id=partner, device_id_type=pl.DeviceIdType.MESH)
    pl.semaphore_wait(barrier, len(partners))

    chip, core = {"dp": chip_peer}, {"dp": core_peer}
    above, below = {"tensor": lax.rem(spot + 1, 4)}, {"tensor": lax.rem(spot + 3, 4)}

    def block(ref, j):
        return ref.at[pl.ds(j * rows, rows), :]

    x_chip = remote(tokens, block(x_all, 1), chip)
    x_core = remote(tokens, block(x_all, 2), core)
    x_last = remote(block(x_all, 1), block(x_all, 3), core)
    dy_chip = remote(cotangent, block(dy_all, 1), chip)
    dy_core = remote(cotangent, block(dy_all, 2), core)
    dy_last = remote(block(dy_all, 1), block(dy_all, 3), core)
    x_chip.start()
    x_core.start()
    dy_core.start()
    x_all[0:rows, :] = tokens[...]
    dy_all[0:rows, :] = cotangent[...]

    def backward(which, slot):
        def body(at):
            part[which, :, at] = nt(cotangent[...], blocks[slot, at, :]).astype(bf16)

        tiles(features, body)

    def forward(index, slot, first=False):
        def body(at):
            term = nn(gathered[index], blocks[slot, :, at])
            base[:, at] = term if first else base[:, at] + term

        tiles(features, body)

    def add(target, a, b):
        def body(at):
            target[:, at] = (a[:, at].astype(f32) + b[:, at].astype(f32)).astype(bf16)

        tiles(target.shape[1], body)

    up_far = remote(part.at[FAR], up_got.at[0], above)
    down_far = remote(part.at[FAR], down_got.at[0], below)
    up_middle = remote(up_sum.at[0], up_got.at[1], above)
    down_middle = remote(down_sum.at[0], down_got.at[1], below)
    up_near = remote(up_sum.at[1], up_got.at[2], above)
    down_near = remote(down_sum.at[1], down_got.at[2], below)
    up_gather = [
        remote(gathered.at[lax.rem(spot + 4 - k, 4)], gathered.at[lax.rem(spot + 4 - k, 4)], above)
        for k in range(3)
    ]
    down_gather = [
        remote(gathered.at[lax.rem(spot + k, 4)], gathered.at[lax.rem(spot + k, 4)], below)
        for k in range(3)
    ]

    def exchange(kind):
        sides = narrow.at[kind], narrow_pair.at[kind], narrow_all.at[kind]
        pair = remote(sides[0].at[pl.ds(2 * rows, 2 * rows), :], sides[1], core)
        peer = remote(narrow_sum.at[kind], narrow_peer.at[kind], chip)
        spread = [
            remote(narrow_own.at[kind], narrow_got.at[kind, k - 1], {"tensor": lax.rem(spot + k, 4)})
            for k in (1, 2, 3)
        ]
        all_chip = remote(block(sides[2], 0), block(sides[2], 1), chip)
        all_core = remote(block(sides[2], 0), block(sides[2], 2), core)
        all_last = remote(block(sides[2], 1), block(sides[2], 3), core)
        return pair, peer, spread, all_chip, all_core, all_last

    def send_peer(kind, steps):
        pair, peer = steps[:2]
        pair.wait_recv()
        narrow_sum[kind] = narrow[kind, rows : 2 * rows, :] + narrow_pair[kind, rows : 2 * rows, :]
        peer.start()

    def send_spread(kind, steps):
        peer, spread = steps[1:3]
        peer.wait_recv()
        narrow_own[kind] = (
            narrow[kind, 0:rows, :] + narrow_pair[kind, 0:rows, :] + narrow_peer[kind]
        )
        for copy in spread:
            copy.start()

    def send_total(kind, steps):
        _, _, spread, all_chip, all_core, _ = steps
        for copy in spread:
            copy.wait_recv()
        total = narrow_own[kind].astype(f32)
        for k in range(3):
            total = total + narrow_got[kind, k].astype(f32)
        narrow_all[kind, 0:rows, :] = total.astype(bf16)
        all_chip.start()
        all_core.start()

    def send_last(steps):
        steps[3].wait_recv()
        steps[5].start()

    def wait_all(steps):
        steps[4].wait_recv()
        steps[5].wait_recv()

    def pass_on(k):
        @pl.when(spot >= k)
        def _():
            up_gather[k - 1].wait_recv()

        @pl.when(spot <= 3 - k)
        def _():
            down_gather[k - 1].wait_recv()

        if k < 3:
            pl.when((spot >= k) & (spot < 3))(up_gather[k].start)
            pl.when((spot <= 3 - k) & (spot > 0))(down_gather[k].start)

    u_steps, g_steps = exchange(0), exchange(1)
    second = pl.ds(2 * rows, 2 * rows)
    out_core = remote(out_delta.at[second, :], out_pair, core)
    back_core = remote(back_delta.at[second, :], back_pair, core)
    out_chip = remote(out_sum, out_peer, chip)
    back_chip = remote(back_sum, back_peer, chip)

    far_load.wait()
    backward(FAR, 0)
    pl.when(spot == 0)(up_far.start)
    pl.when(spot == 3)(down_far.start)
    own_load.start()

    def iota(shape, axis):
        return lax.broadcasted_iota(jnp.int32, shape, axis)

    def total_of(mask, values, axis):
        return jnp.sum(jnp.where(mask, values, 0.0), axis=axis, keepdims=True)

    micros = destination.shape[0]
    per_group = micros // 4
    width = 4 * rows
    first, later = iota((micros, micros), 0), iota((micros, micros), 1)
    to_column = destination[...].astype(f32)
    to_row = total_of(first == later, to_column, 0)
    shares = (first // per_group == later // per_group) & (to_column == to_row)
    place_column = total_of(shares & (later < first), 1.0, 1)
    place_row = total_of(shares & (first < later), 1.0, 0)
    source_column = (iota((micros, 1), 0) // per_group * CAP).astype(f32)
    source_row = (iota((1, micros), 1) // per_group * CAP).astype(f32)
    target_column = to_column * (4.0 * CAP) + source_column + place_column
    target_row = to_row * (4.0 * CAP) + source_row + place_row
    last_peer = lax.rem(core_peer + 2, 4)

    def unit(index):
        j = index // rows
        peer = jnp.where(
            j == 0, me, jnp.where(j == 1, chip_peer, jnp.where(j == 2, core_peer, last_peer))
        )
        return peer * (rows // MICRO_TOKENS) + lax.rem(index, rows) // MICRO_TOKENS

    row_ids, column_ids = iota((width, 1), 0), iota((1, width), 1)
    row_unit, column_unit = unit(row_ids), unit(column_ids)
    row_place, column_place = lax.rem(row_ids, MICRO_TOKENS), lax.rem(column_ids, MICRO_TOKENS)
    column_target = total_of(iota((micros, width), 0) == column_unit, target_column, 0)
    move[...] = jnp.where(
        (row_unit.astype(f32) == column_target) & (row_place == column_place), 1.0, 0.0
    ).astype(bf16)
    home_micro = jnp.zeros((1, micros), f32)
    own_bucket = jnp.int32(0)
    for a in range(home_row.shape[0]):
        home_micro = home_micro + jnp.where(adapter[...] == a, home_row[a].astype(f32), 0.0)
        own_bucket = own_bucket + jnp.where(home_row[a] == me, bucket[a], 0)
    chosen = row_unit.astype(f32) == target_row
    counted = total_of(chosen, live_count[...].astype(f32), 1)
    live = row_place.astype(f32) < counted
    home_here = total_of(chosen, home_micro, 1)
    self_id = me.astype(f32)
    mine = jnp.where(live & (home_here == self_id), 1.0, 0.0)
    own_live = jnp.where(live, 1.0, 0.0)[0:rows, :]
    micro_home = total_of(iota((width, micros), 1) == row_unit, home_micro, 1)
    micro_mine = jnp.where(micro_home == self_id, 1.0, 0.0)
    kept = RANK_LOW * jnp.where(own_bucket == 0, 1, jnp.where(own_bucket == 1, 4, 16))
    columns = jnp.where(iota((1, rank), 1) < kept, 1.0, 0.0)
    scale = jnp.where(own_bucket == 0, 4.0, jnp.where(own_bucket == 1, 2.0, 1.0))

    middle_load.wait()
    backward(MIDDLE, 1)
    x_chip.wait_recv()
    x_last.start()
    dy_chip.start()
    x_core.wait_recv()
    x_last.wait_recv()

    def pack(at):
        gathered[spot, :, at] = nn(move[0:rows, :], x_all[:, at]).astype(bf16)

    tiles(features, pack)
    pl.when(spot < 3)(up_gather[0].start)
    pl.when(spot > 0)(down_gather[0].start)
    narrow[0] = (nn(x_all[...], down[...]) * micro_mine).astype(bf16)
    u_steps[0].start()
    near_load.wait()
    backward(NEAR, 2)
    send_peer(0, u_steps)
    own_load.wait()
    backward(OWN, 0)
    send_spread(0, u_steps)
    forward(spot, 0, first=True)
    dy_chip.wait_recv()
    dy_last.start()
    dy_core.wait_recv()
    dy_last.wait_recv()
    narrow[1] = (nt(dy_all[...], up[...]) * mine).astype(bf16)
    g_steps[0].start()
    pass_on(1)

    @pl.when(spot == 0)
    def _():
        up_sum[0] = part[MIDDLE]
        up_middle.start()

    @pl.when(spot == 3)
    def _():
        down_sum[0] = part[MIDDLE]
        down_middle.start()

    send_peer(1, g_steps)
    send_total(0, u_steps)
    send_spread(1, g_steps)
    send_last(u_steps)
    forward(near_index, 2)
    again_load.start()
    wait_all(u_steps)
    low_source = (narrow_all[0].astype(f32) * columns).astype(bf16)
    low_wide = nn(move[...], low_source) * mine
    low = low_wide.astype(bf16)

    def out_part(at):
        out_delta[:, at] = (scale * nn(low, up[:, at])).astype(bf16)

    tiles(features, out_part)
    out_core.start()
    out_core.wait_recv()
    add(out_sum, block(out_delta, 1), block(out_pair, 1))
    out_chip.start()
    pass_on(2)

    @pl.when(spot == 1)
    def _():
        up_far.wait_recv()
        add(up_sum.at[0], part.at[MIDDLE], up_got.at[0])
        up_middle.start()

    @pl.when(spot == 2)
    def _():
        down_far.wait_recv()
        add(down_sum.at[0], part.at[MIDDLE], down_got.at[0])
        down_middle.start()

    @pl.when(spot == 0)
    def _():
        up_sum[1] = part[NEAR]
        up_near.start()

    @pl.when(spot == 3)
    def _():
        down_sum[1] = part[NEAR]
        down_near.start()

    send_total(1, g_steps)
    send_last(g_steps)
    wait_all(g_steps)
    grad_low_wide = narrow_all[1].astype(f32) * (columns * scale) * mine
    grad_low = grad_low_wide.astype(bf16)

    def back_part(at):
        back_delta[:, at] = nt(grad_low, down[at, :]).astype(bf16)

    tiles(features, back_part)
    back_core.start()
    forward(middle_index, 1)
    back_core.wait_recv()
    add(back_sum, block(back_delta, 1), block(back_pair, 1))
    back_chip.start()

    @pl.when(spot == 1)
    def _():
        up_middle.wait_recv()
        add(up_sum.at[1], part.at[NEAR], up_got.at[1])
        up_near.start()
        down_middle.wait_recv()
        add(down_sum.at[1], part.at[FAR], down_got.at[1])
        down_near.start()

    @pl.when(spot == 2)
    def _():
        down_middle.wait_recv()
        add(down_sum.at[1], part.at[NEAR], down_got.at[1])
        down_near.start()
        up_middle.wait_recv()
        add(up_sum.at[1], part.at[FAR], up_got.at[1])
        up_near.start()

    low_turned = low_wide.T.astype(bf16)
    grad_turned = nn(grad_low_wide.T.astype(bf16), move[...]).astype(bf16)

    def gradients(at):
        grad_b[:, at] = (scale * nn(low_turned, dy_all[:, at])).astype(bf16)
        grad_a[at, :] = nn(grad_turned, x_all[:, at]).T.astype(bf16)

    tiles(features, gradients)
    pass_on(3)
    again_load.wait()
    forward(far_index, 2)
    out_chip.wait_recv()

    def finish_out(at):
        delta = out_delta[0:rows, at].astype(f32) + out_pair[0:rows, at].astype(f32)
        delta = delta + out_peer[:, at].astype(f32)
        outputs[:, at] = (own_live * (base[:, at] + delta)).astype(bf16)

    tiles(features, finish_out)
    base[...] = part[OWN].astype(f32)

    @pl.when(spot > 0)
    def _():
        up_near.wait_recv()
        base[...] = base[...] + up_got[2].astype(f32)

    @pl.when(spot < 3)
    def _():
        down_near.wait_recv()
        base[...] = base[...] + down_got[2].astype(f32)

    back_chip.wait_recv()

    def finish_back(at):
        delta = back_delta[0:rows, at].astype(f32) + back_pair[0:rows, at].astype(f32)
        delta = delta + back_peer[:, at].astype(f32)
        input_gradient[:, at] = (own_live * (base[:, at] + delta)).astype(bf16)

    tiles(features, finish_back)

    for copy in (x_chip, x_core, x_last, dy_chip, dy_core, dy_last):
        copy.wait_send()
    for pair, peer, spread, *rest in (u_steps, g_steps):
        for copy in (pair, peer, *spread, *rest):
            copy.wait_send()
    for copy in (out_core, out_chip, back_core, back_chip):
        copy.wait_send()
    pl.when(spot == 0)(up_far.wait_send)
    pl.when(spot == 3)(down_far.wait_send)
    pl.when(spot < 2)(up_middle.wait_send)
    pl.when(spot >= 2)(down_middle.wait_send)
    pl.when(spot < 3)(up_near.wait_send)
    pl.when(spot > 0)(down_near.wait_send)
    for k in range(3):
        pl.when((spot >= k) & (spot < 3))(up_gather[k].wait_send)
        pl.when((spot <= 3 - k) & (spot > 0))(down_gather[k].wait_send)


def layer(tokens, cotangent, weight, down, up, *rest):
    rows, features = tokens.shape
    rank = down.shape[1]
    bf16 = jnp.bfloat16

    def held(*shape):
        return pltpu.VMEM(shape, bf16)

    vmem = pl.BlockSpec(memory_space=pltpu.VMEM)
    smem = pl.BlockSpec(memory_space=pltpu.SMEM)
    all_rows = 4 * rows
    return pl.pallas_call(
        layer_kernel,
        out_shape=(
            jax.ShapeDtypeStruct((rows, features), bf16),
            jax.ShapeDtypeStruct((rows, features), bf16),
            jax.ShapeDtypeStruct((features, rank), bf16),
            jax.ShapeDtypeStruct((rank, features), bf16),
        ),
        in_specs=[vmem, vmem, pl.BlockSpec(memory_space=pl.ANY)] + [vmem] * 5 + [smem] * 2,
        out_specs=(vmem,) * 4,
        scratch_shapes=[
            held(all_rows, features),
            held(all_rows, features),
            held(4, rows, features),
            held(4, rows, features),
            held(3, rows, features),
            held(3, rows, features),
            held(2, rows, features),
            held(2, rows, features),
            held(3, features, features),
            held(all_rows, all_rows),
            held(2, all_rows, rank),
            held(2, 2 * rows, rank),
            held(2, rows, rank),
            held(2, rows, rank),
            held(2, rows, rank),
            held(2, 3, rows, rank),
            held(2, all_rows, rank),
            held(all_rows, features),
            held(2 * rows, features),
            held(rows, features),
            held(rows, features),
            held(all_rows, features),
            held(2 * rows, features),
            held(rows, features),
            held(rows, features),
            pltpu.VMEM((rows, features), jnp.float32),
            pltpu.SemaphoreType.DMA((5,)),
            pltpu.SemaphoreType.DMA((48,)),
            pltpu.SemaphoreType.DMA((48,)),
        ],
        compiler_params=pltpu.CompilerParams(
            collective_id=0, has_side_effects=True, vmem_limit_bytes=60 * 1024 * 1024
        ),
        name="layer",
    )(tokens, cotangent, weight, down, up, *rest)


def hand_on_kernel(count, *refs):
    sources, results = refs[:count], refs[count : 2 * count]
    held, sems = refs[2 * count : 3 * count], refs[3 * count]
    loads = [
        pltpu.make_async_copy(sources[i], held[i], sems.at[2 * i]) for i in range(count)
    ]
    stores = [
        pltpu.make_async_copy(held[i], results[i], sems.at[2 * i + 1]) for i in range(count)
    ]
    for copy in loads:
        copy.start()
    for load, store in zip(loads, stores):
        load.wait()
        store.start()
    for copy in stores:
        copy.wait()


def handed_on(*arrays):
    anywhere = pl.BlockSpec(memory_space=pltpu.HBM)
    count = len(arrays)
    return pl.pallas_call(
        functools.partial(hand_on_kernel, count),
        out_shape=tuple(jax.ShapeDtypeStruct(a.shape, a.dtype) for a in arrays),
        in_specs=[anywhere] * count,
        out_specs=(anywhere,) * count,
        scratch_shapes=[pltpu.VMEM(a.shape, a.dtype) for a in arrays]
        + [pltpu.SemaphoreType.DMA((2 * count,))],
        compiler_params=pltpu.CompilerParams(vmem_limit_bytes=32 * 1024 * 1024),
        name="hand_on",
    )(*arrays)


def local(
    tokens,
    weight,
    adapter_down_factor,
    adapter_up_factor,
    cotangent,
    micro_destination_group,
    micro_adapter,
    micro_token_count,
    adapter_rank_bucket,
    adapter_home_row,
):
    n = lax.axis_size("dp")
    me = lax.axis_index("dp")
    n_tensor = lax.axis_size("tensor")
    features = tokens.shape[1]
    own_rows = cotangent.shape[0]
    f32, bf16 = jnp.float32, jnp.bfloat16
    down, up = adapter_down_factor[0], adapter_up_factor[0]
    if n == 4 and n_tensor == 4 and tokens.shape == cotangent.shape:
        outputs, input_gradient, grad_a, grad_b = handed_on(
            *layer(
                tokens, cotangent, weight, down, up, micro_destination_group,
                micro_adapter.reshape(1, -1), micro_token_count.reshape(1, -1),
                adapter_rank_bucket, adapter_home_row,
            )
        )
        return outputs, input_gradient, grad_a[None], grad_b[None]

    micro_target, micro_home, slot_ids, home, counted = packing(
        micro_destination_group, micro_adapter, micro_token_count, adapter_home_row, n, me
    )
    token = jnp.arange(tokens.shape[0] * n, dtype=jnp.int32) % MICRO_TOKENS
    place = jnp.arange(own_rows * n, dtype=jnp.int32) % MICRO_TOKENS
    move = (
        (rows_of(slot_ids) * MICRO_TOKENS + place)[:, None]
        == (rows_of(micro_target) * MICRO_TOKENS + token)[None, :]
    ).astype(bf16)
    live = place < rows_of(counted)
    mine = (live & (rows_of(home) == me)).astype(f32)[:, None]
    micro_mine = (rows_of(micro_home) == me).astype(f32)[:, None]
    own_live = live[:own_rows].astype(f32)[:, None]
    bucket = jnp.sum(jnp.where(adapter_home_row == me, adapter_rank_bucket, 0))
    rank = RANK_LOW * jnp.where(bucket == 0, 1, jnp.where(bucket == 1, 4, 16))
    scale = jnp.sqrt(LARGEST_RANK / rank.astype(f32))
    columns = (jnp.arange(LARGEST_RANK, dtype=jnp.int32) < rank).astype(f32)[None, :]

    x_all = gather_blocks(tokens, n)
    dy_all = gather_blocks(cotangent, n)

    back_part = lax.dot_general(
        weight, cotangent, (((1,), (1,)), ((), ())), preferred_element_type=f32
    ).astype(bf16)
    back = lax.psum_scatter(back_part, "tensor", scatter_dimension=0, tiled=True).T

    x_own = jnp.dot(move[:own_rows], x_all, preferred_element_type=f32).astype(bf16)
    x_full = lax.all_gather(x_own, "tensor", axis=1, tiled=True)
    base = jnp.dot(x_full, weight, preferred_element_type=f32)

    u_part = jnp.dot(x_all, down, preferred_element_type=f32).astype(bf16)
    g_part = lax.dot_general(
        dy_all, up, (((1,), (1,)), ((), ())), preferred_element_type=f32
    ).astype(bf16)
    u_sum, g_sum = lax.psum(u_part, "tensor"), lax.psum(g_part, "tensor")

    low_source = (u_sum.astype(f32) * columns).astype(bf16)
    low = (jnp.dot(move, low_source, preferred_element_type=f32) * mine).astype(bf16)
    grad_low = (g_sum.astype(f32) * columns * scale * mine).astype(bf16)
    grad_low_source = lax.dot_general(
        move, grad_low, (((0,), (0,)), ((), ())), preferred_element_type=f32
    ).astype(bf16)

    out_delta = (scale * jnp.dot(low, up, preferred_element_type=f32)).astype(bf16)
    out_delta = reduce_blocks(out_delta, n)
    back_delta = lax.dot_general(
        grad_low, down, (((1,), (1,)), ((), ())), preferred_element_type=f32
    ).astype(bf16)
    back_delta = reduce_blocks(back_delta, n)

    grad_a = lax.dot_general(
        x_all, grad_low_source, (((0,), (0,)), ((), ())), preferred_element_type=f32
    )
    grad_b = scale * lax.dot_general(
        low, dy_all, (((0,), (0,)), ((), ())), preferred_element_type=f32
    )
    outputs = own_live * (base + out_delta.astype(f32))
    input_gradient = own_live * (back.astype(f32) + back_delta.astype(f32))
    return (
        outputs.astype(bf16),
        input_gradient.astype(bf16),
        grad_a.astype(bf16)[None],
        grad_b.astype(bf16)[None],
    )


def solution(mesh):
    in_specs = (
        P(("parts", "dp"), "tensor"),
        P(None, "tensor"),
        P(("parts", "dp"), "tensor", None),
        P(("parts", "dp"), None, "tensor"),
        P(("parts", "dp"), "tensor"),
        P("parts", None),
        P("parts"),
        P("parts"),
        P("parts"),
        P("parts"),
    )
    out_specs = (
        P(("parts", "dp"), "tensor"),
        P(("parts", "dp"), "tensor"),
        P(("parts", "dp"), "tensor", None),
        P(("parts", "dp"), None, "tensor"),
    )
    return jax.shard_map(local, mesh=mesh, in_specs=in_specs, out_specs=out_specs, check_vma=False)
```
